256 devices in a mesh: ctx: 128 (over y, z, x), kvh: 2 (over core).
Axes of the slice: x: 4, y: 4, z: 8, core: 2. Of those that a mesh axis runs over, the one named last changes fastest.
Arguments:
- queries: bfloat16 [32768, 4096], P('ctx', 'kvh'), may hold values from -8 to 8
- current_keys: bfloat16 [32768, 1024], P('ctx', 'kvh'), may hold values from -8 to 8
- current_values: bfloat16 [32768, 1024], P('ctx', 'kvh'), may hold values from -6 to 6
- cached_key_pages: bfloat16 [524288, 1024], P('ctx', 'kvh'), may hold values from -8 to 8
- cached_value_pages: bfloat16 [524288, 1024], P('ctx', 'kvh'), may hold values from -6 to 6
- picks: int32 [128, 32, 3], P('ctx', 'kvh'), may hold values from 0 to 1023, as said below
Outputs:
- attended: bfloat16 [32768, 4096], P('ctx', 'kvh')
The draws below stay inside these ranges and needn't reach their ends.
Inputs may be any that keep to these rules, and one draw needn't show every extreme that they name: Block n of the cache belongs to owner n // 8. For one query block and one set of 16 consecutive heads (h // 16 fixed), at most 1 of its 48 picks belong to one owner, and for each such set of heads one owner holds exactly 1 picks of every query block. The 3 picks of one query block and head belong to different owners.
All inputs are finite; a program needn't handle non-finite values.
Results may differ from the reference program's by a relative error of at most 0.0055.
Values may be sent and summed in bfloat16 or wider, within the bound.
A program may use at most 128 MiB of HBM per device.

```python
import jax
import jax.numpy as jnp
from jax import lax

QUERY_HEADS = 32
KEY_VALUE_HEADS = 8
HEAD_SIZE = 128
KEY_BLOCK_SIZE = 512
TOPK = 3
CB_DEV = 8
QUERY_BLOCK_SIZE = 256
HQ_DEV = 16
NQB = 128
KEY_BLOCK_COUNT = 1024
STRETCH_LENGTH = 32768
CACHE_POSITIONS = 524288


def drawn_rows(key, shape):
    return jnp.clip(jax.random.normal(key, shape, jnp.float32), -6.0, 6.0)


def draw_queries(key, part):
    key = jax.random.fold_in(key, 11)
    return drawn_rows(key, (STRETCH_LENGTH, QUERY_HEADS * HEAD_SIZE)).astype(jnp.bfloat16)


def draw_current_keys(key, part):
    key = jax.random.fold_in(key, 23)
    return drawn_rows(key, (STRETCH_LENGTH, KEY_VALUE_HEADS * HEAD_SIZE)).astype(jnp.bfloat16)


def draw_cached_key_pages(key, part):
    key = jax.random.fold_in(key, 37)
    return drawn_rows(key, (CACHE_POSITIONS, KEY_VALUE_HEADS * HEAD_SIZE)).astype(jnp.bfloat16)


def draw_picks(key, part):
    key = jax.random.fold_in(key, 53)
    halves = QUERY_HEADS // HQ_DEV

    def one(block, half):
        hot = jax.random.randint(jax.random.fold_in(jax.random.fold_in(key, 1), half), (), 0, NQB)
        local = jax.random.fold_in(jax.random.fold_in(jax.random.fold_in(key, 2), block), half)
        first_key, second_key, third_key = jax.random.split(local, 3)
        others = jax.random.permutation(first_key, NQB - 1)
        order = jnp.concatenate([hot[None], (hot + 1 + others) % NQB])
        head_order = jax.random.permutation(second_key, HQ_DEV)
        position = head_order[:, None] * TOPK + jnp.arange(TOPK)[None, :]
        owner_of = order[position % NQB]
        within = jax.random.randint(third_key, (HQ_DEV, TOPK), 0, CB_DEV)
        return (owner_of * CB_DEV + within).astype(jnp.int32)
    inner = jax.vmap(one, in_axes=(None, 0))
    outer = jax.vmap(inner, in_axes=(0, None))
    table = outer(jnp.arange(NQB), jnp.arange(halves))
    return table.reshape(NQB, QUERY_HEADS, TOPK)


def steps_of(key, dims, shards, low, high):
    loudness = 1.0
    for dim, parts in shards:
        heights = jax.random.uniform(jax.random.fold_in(jax.random.fold_in(key, 6), dim), (parts,), jnp.float32, low / len(shards), high / len(shards))
        loudness = loudness * jnp.repeat(jnp.exp(heights), dims[dim] // parts).reshape((-1,) + (1,) * (len(dims) - 1 - dim))
    return loudness


def bell_draw(rng, dims, width, limit, shards=(), kind=jnp.bfloat16):
    entries = width * jax.random.normal(rng, dims, jnp.float32)
    if shards:
        entries = entries * steps_of(rng, dims, shards, -0.22, 0.18)
    return jnp.clip(entries, -limit, limit).astype(kind)


def setup_inputs(seed: int = 0) -> dict:
    streams_of = jax.random.split(jax.random.key(seed), 7)
    queries = draw_queries(jax.random.fold_in(streams_of[6], 71), 0)
    current_keys = draw_current_keys(jax.random.fold_in(streams_of[6], 71), 0)
    current_values = bell_draw(streams_of[2], (STRETCH_LENGTH, KEY_VALUE_HEADS * HEAD_SIZE), 1.0, 6.0, ((0, 128), (1, 2)))
    cached_key_pages = draw_cached_key_pages(jax.random.fold_in(streams_of[6], 71), 0)
    cached_value_pages = bell_draw(streams_of[4], (CACHE_POSITIONS, KEY_VALUE_HEADS * HEAD_SIZE), 1.0, 6.0, ((0, 128), (1, 2)))
    picks = draw_picks(jax.random.fold_in(streams_of[6], 71), 0)
    return {"queries": queries, "current_keys": current_keys, "current_values": current_values, "cached_key_pages": cached_key_pages, "cached_value_pages": cached_value_pages, "picks": picks}


def round_bf16(value):
    return lax.optimization_barrier(value.astype(jnp.bfloat16)).astype(jnp.float32)


def reference(queries, current_keys, current_values, cached_key_pages, cached_value_pages, picks):
    query_group_width = QUERY_HEADS // KEY_VALUE_HEADS
    score_scale = HEAD_SIZE ** -0.5
    cache_key_rows = cached_key_pages.reshape(KEY_BLOCK_COUNT, KEY_BLOCK_SIZE, KEY_VALUE_HEADS, HEAD_SIZE)
    cache_value_rows = cached_value_pages.reshape(KEY_BLOCK_COUNT, KEY_BLOCK_SIZE, KEY_VALUE_HEADS, HEAD_SIZE)
    stretch_key_rows = current_keys.reshape(STRETCH_LENGTH // KEY_BLOCK_SIZE, KEY_BLOCK_SIZE, KEY_VALUE_HEADS, HEAD_SIZE)
    stretch_value_rows = current_values.reshape(STRETCH_LENGTH // KEY_BLOCK_SIZE, KEY_BLOCK_SIZE, KEY_VALUE_HEADS, HEAD_SIZE)
    head_kv = (jnp.arange(QUERY_HEADS) // query_group_width).astype(jnp.int32)

    def one_block(block):
        query_block = lax.dynamic_slice_in_dim(queries, block * QUERY_BLOCK_SIZE, QUERY_BLOCK_SIZE, 0).reshape(QUERY_BLOCK_SIZE, QUERY_HEADS, HEAD_SIZE).astype(jnp.float32)
        chosen = picks[block]
        key_pick = cache_key_rows[chosen, :, head_kv[:, None], :].astype(jnp.float32)
        value_pick = cache_value_rows[chosen, :, head_kv[:, None], :].astype(jnp.float32)
        pick_scores = jnp.einsum('qhd,htkd->htqk', query_block, key_pick) * score_scale
        pick_max = jnp.max(pick_scores, axis=-1)
        pick_weights = jnp.exp(pick_scores - pick_max[..., None])
        pick_total = jnp.sum(pick_weights, axis=-1)
        pick_rounded = round_bf16(pick_weights)
        pick_out = jnp.einsum('htqk,htkd->htqd', pick_rounded, value_pick) / pick_total[..., None]
        pick_out = round_bf16(pick_out)
        own_k = stretch_key_rows[block // 2][:, head_kv, :].astype(jnp.float32)
        own_v = stretch_value_rows[block // 2][:, head_kv, :].astype(jnp.float32)
        own_scores = jnp.einsum('qhd,khd->hqk', query_block, own_k) * score_scale
        query_pos = (block % 2) * QUERY_BLOCK_SIZE + jnp.arange(QUERY_BLOCK_SIZE)
        key_pos = jnp.arange(KEY_BLOCK_SIZE)
        visible = key_pos[None, :] <= query_pos[:, None]
        own_scores = jnp.where(visible[None], own_scores, -jnp.inf)
        own_max = jnp.max(own_scores, axis=-1)
        own_weights = jnp.where(visible[None], jnp.exp(own_scores - own_max[..., None]), 0.0)
        own_total = jnp.sum(own_weights, axis=-1)
        own_rounded = round_bf16(own_weights)
        own_out = jnp.einsum('hqk,khd->hqd', own_rounded, own_v) / own_total[..., None]
        overall = jnp.maximum(own_max, jnp.max(pick_max, axis=1))
        own_weight = own_total * jnp.exp(own_max - overall)
        pick_weight = pick_total * jnp.exp(pick_max - overall[:, None])
        numer = own_weight[..., None] * own_out + jnp.sum(pick_weight[..., None] * pick_out, axis=1)
        result = numer / (own_weight + jnp.sum(pick_weight, axis=1))[..., None]
        return result.transpose(1, 0, 2).reshape(QUERY_BLOCK_SIZE, QUERY_HEADS * HEAD_SIZE).astype(jnp.bfloat16)

    blocks_out = lax.map(one_block, jnp.arange(NQB, dtype=jnp.int32))
    return blocks_out.reshape(STRETCH_LENGTH, QUERY_HEADS * HEAD_SIZE)
```

```python
import functools

import jax
import jax.numpy as jnp
from jax import lax
from jax.experimental import pallas as pl
from jax.experimental.pallas import tpu as pltpu
from jax.sharding import PartitionSpec as P

HEAD_SIZE = 128
KEY_BLOCK_SIZE = 512
TOPK = 3
MESH = pl.DeviceIdType.MESH
NX, NY, NZ = 4, 4, 8
PLANE = NX * NY
HEADS = 16
KV = 4
GROUP = HEADS // KV
OWNED = 8
ROWS = 256
HALF = 128
OWNERS = 128
SCALE = HEAD_SIZE**-0.5
SCALE2 = SCALE * 1.4426950408889634
LOW = -1e30


def kernel(*refs):
    (q_ref, ck_ref, cv_ref, kp_ref, vp_ref, code_ref, out_ref), refs = refs[:7], refs[7:]
    zq, refs = [refs[2 * s : 2 * s + 2] for s in range(NZ)], refs[2 * NZ :]
    ret, refs = [refs[2 * s : 2 * s + 2] for s in range(NZ)], refs[2 * NZ :]
    rl, refs = refs[:NZ], refs[NZ:]
    (
        kbuf, vstage, vbuf, tx, rx, lout, zacc, zl, own_o, own_l, pk, pvt, cvt, lt, wt,
        zcode, pcode, zsm, rsm,
        k_sem, v_sem, zq_send, zq_recv, zc_send, zc_recv, pc_send, pc_recv, sm_sem,
        xp_send, xp_recv, tx_send, rx_recv, rs_send, rs_recv, ls_send, ls_recv,
        za_send, za_recv, zl_send, zl_recv,
    ) = refs
    me = lax.axis_index("ctx")
    core = lax.axis_index("kvh")
    x = lax.rem(me, NX)
    z = lax.rem(me // NX, NZ)
    y = me // (NX * NZ)

    def in_plane(k):
        return (
            lax.rem(y + k // NX, NY) * (NX * NZ) + z * NX + lax.rem(x + lax.rem(k, NX), NX),
            core,
        )

    def opposite(k):
        return (
            lax.rem(y + NY - k // NX, NY) * (NX * NZ)
            + z * NX
            + lax.rem(x + NX - lax.rem(k, NX), NX),
            core,
        )

    def along_z(d):
        return (y * (NX * NZ) + lax.rem(z + d + NZ, NZ) * NX + x, core)

    def owner_at(k):
        return in_plane(k)[0]

    def remote(src, dst, send, recv, device):
        return pltpu.make_async_remote_copy(
            src_ref=src,
            dst_ref=dst,
            send_sem=send,
            recv_sem=recv,
            device_id=device,
            device_id_type=MESH,
        )

    def key_copy(v):
        return pltpu.make_async_copy(
            kp_ref.at[:, :, pl.ds(v * HEAD_SIZE, HEAD_SIZE)],
            kbuf.at[pl.ds(v * OWNED, OWNED)],
            k_sem.at[v],
        )

    def value_copy(v):
        return pltpu.make_async_copy(
            vp_ref.at[:, :, pl.ds(v * HEAD_SIZE, HEAD_SIZE)], vstage.at[v % 2], v_sem.at[v]
        )

    value_copy(0).start()
    value_copy(1).start()
    for v in range(KV):
        key_copy(v).start()

    barrier = pltpu.get_barrier_semaphore()
    for k in range(1, PLANE):
        pl.semaphore_signal(barrier, inc=1, device_id=in_plane(k), device_id_type=MESH)
    for d in range(1, NZ):
        pl.semaphore_signal(barrier, inc=1, device_id=along_z(d), device_id_type=MESH)
    pl.semaphore_wait(barrier, PLANE - 1 + NZ - 1)

    zcode[0] = code_ref[...]

    def z_code(d):
        return remote(zcode.at[0], zcode.at[d], zc_send, zc_recv, along_z(d))

    for d in range(1, NZ):
        z_code(d).start()

    def z_query(s, c, to, step):
        return remote(
            zq[s][c], zq[to][c], zq_send.at[0 if step > 0 else 1, s, c], zq_recv.at[to, c],
            along_z(step),
        )

    for c in range(2):
        for h in range(HEADS):
            zq[0][c][h] = q_ref[
                c * HALF : (c + 1) * HALF, h * HEAD_SIZE : (h + 1) * HEAD_SIZE
            ].T
        z_query(0, c, 1, 1).start()
        z_query(0, c, NZ - 1, -1).start()

    for v in range(KV):
        cvt[v] = cv_ref[:, v * HEAD_SIZE : (v + 1) * HEAD_SIZE].T
    odd = lax.rem(me, 2)
    partner = (me + 1 - 2 * odd, core)
    pair = [
        remote(ck_ref, pk, xp_send.at[0], xp_recv.at[0], partner),
        remote(cvt, pvt, xp_send.at[1], xp_recv.at[1], partner),
    ]
    for copy in pair:
        copy.start()

    z_codes = remote(
        zcode.at[pl.ds(1, NZ - 1)], zcode.at[pl.ds(1, NZ - 1)], zc_send, zc_recv, along_z(1)
    )
    z_codes.wait_recv()

    def p_code(k):
        return remote(
            zcode.at[:, :, pl.ds(0, OWNERS)], pcode.at[k], pc_send, pc_recv, in_plane(k)
        )

    def start_p_code(k, _):
        p_code(k).start()
        return 0

    lax.fori_loop(1, PLANE, start_p_code, 0)
    pcode[0] = zcode[:, :, :OWNERS]
    z_to_smem = pltpu.make_async_copy(zcode, zsm, sm_sem.at[0])
    z_to_smem.start()
    z_to_smem.wait()

    def query_copy(s, c, k):
        return remote(
            tx.at[s, c, k], rx.at[s, c, k], tx_send.at[s], rx_recv.at[s, c, k], in_plane(k)
        )

    def send_out(s, c):
        first = lax.rem(zsm[s, 0, owner_at(0)], HEADS)
        rx[s, c, 0] = zq[s][c][first]

        def body(k, _):
            head = lax.rem(zsm[s, 0, owner_at(k)], HEADS)
            tx[s, c, k] = zq[s][c][head]
            query_copy(s, c, k).start()
            return 0

        lax.fori_loop(1, PLANE, body, 0)

    def pass_on(s, c):
        remote(zq[s][c], zq[s][c], zq_send.at[0, s, c], zq_recv.at[s, c], along_z(1)).wait_recv()
        if s < NZ // 2 - 1 or (s == NZ // 2 - 1 and c == 0):
            z_query(s, c, s + 1, 1).start()
        elif s > NZ // 2 + 1 or (s == NZ // 2 + 1 and c == 1):
            z_query(s, c, s - 1, -1).start()

    def arrive(*pairs):
        for s, c in pairs:
            pass_on(s, c)
        for s, c in pairs:
            send_out(s, c)

    def attend(keys, queries, values):
        scores = jnp.dot(keys, queries, preferred_element_type=jnp.float32)
        top = jnp.max(scores, axis=0, keepdims=True)
        weights = jnp.exp2(scores * SCALE2 - top * SCALE2)
        total = jnp.sum(weights, axis=0, keepdims=True)
        out = jnp.dot(values, weights.astype(jnp.bfloat16), preferred_element_type=jnp.float32)
        return out * (1.0 / total), top * SCALE + jnp.log(total)

    def unit(s, k):
        table = lax.div(rsm[k, s, 0, me], HEADS)
        queries = jnp.concatenate([rx[s, 0, k], rx[s, 1, k]], axis=1)
        out, level = attend(kbuf[table], queries, vbuf[table])
        out = out.astype(jnp.bfloat16)
        rx[s, 0, k] = out[:, :HALF]
        rx[s, 1, k] = out[:, HALF:]
        lout[s, k] = level

    def back_copy(s, c, k):
        return remote(
            rx.at[s, c, k], ret[s][c].at[k], rs_send.at[s], rs_recv.at[s, c], opposite(k)
        )

    def level_copy(s, k):
        return remote(lout.at[s, k], rl[s].at[k], ls_send.at[s], ls_recv.at[s], opposite(k))

    def units(a, b, count, then=None):
        def body(j, _):
            s = a + (b - a) * lax.div(j, PLANE // 2)
            for i in range(2):
                k = lax.rem(j, PLANE // 2) * 2 + i

                def wait(k=k):
                    query_copy(s, 0, k).wait_recv()
                    query_copy(s, 1, k).wait_recv()

                if i == 0:
                    pl.when(k > 0)(wait)
                else:
                    wait()
            for i in range(2):
                unit(s, lax.rem(j, PLANE // 2) * 2 + i)
            if then is not None:
                for i in range(2):
                    then(lax.rem(j, PLANE // 2) * 2 + i, i)
            return 0

        lax.fori_loop(0, count * PLANE // 2, body, 0)
        for s in (a, b)[:count]:
            for c in range(2):
                ret[s][c][0] = rx[s, c, 0]
            rl[s][0] = lout[s, 0]
            rl[s][PLANE] = jnp.full((1, ROWS), LOW, jnp.float32)

    def send_back(s, c, with_level):
        def body(k, _):
            back_copy(s, c, k).start()
            if with_level:
                level_copy(s, k).start()
            return 0

        lax.fori_loop(1, PLANE, body, 0)

    send_out(0, 0)
    send_out(0, 1)

    for v in range(KV):
        value_copy(v).wait()

        def turn(w, _, v=v):
            vbuf[v * OWNED + w] = vstage[v % 2, w].T
            return 0

        lax.fori_loop(0, OWNED, turn, 0)
        if v + 2 < KV:
            value_copy(v + 2).start()

    arrive((1, 0), (7, 0))

    for copy in pair:
        copy.wait_recv()

    def own(h, _):
        v = h // GROUP
        lanes = pl.ds(pl.multiple_of(v * HEAD_SIZE, HEAD_SIZE), HEAD_SIZE)
        queries = jnp.concatenate([zq[0][0][h], zq[0][1][h]], axis=1)
        before = jnp.dot(pk[:, lanes], queries, preferred_element_type=jnp.float32)
        here = jnp.dot(ck_ref[:, lanes], queries, preferred_element_type=jnp.float32)
        key_pos = lax.broadcasted_iota(jnp.int32, (ROWS, ROWS), 0)
        query_pos = lax.broadcasted_iota(jnp.int32, (ROWS, ROWS), 1)
        before = jnp.where(odd == 1, before, LOW)
        here = jnp.where(key_pos <= query_pos, here, LOW)
        top = jnp.maximum(
            jnp.max(before, axis=0, keepdims=True), jnp.max(here, axis=0, keepdims=True)
        )
        weights_before = jnp.exp2((before - top) * SCALE2)
        weights_here = jnp.exp2((here - top) * SCALE2)
        total = jnp.sum(weights_before, axis=0, keepdims=True) + jnp.sum(
            weights_here, axis=0, keepdims=True
        )
        out = jnp.dot(pvt[v], weights_before.astype(jnp.bfloat16), preferred_element_type=jnp.float32)
        out += jnp.dot(cvt[v], weights_here.astype(jnp.bfloat16), preferred_element_type=jnp.float32)
        out = out * (1.0 / total)
        level = top * SCALE + jnp.log(total)
        for c in range(2):
            own_o[c, h] = out[:, c * HALF : (c + 1) * HALF]
            own_l[c, pl.ds(h, 1), :] = level[:, c * HALF : (c + 1) * HALF]
        return 0

    lax.fori_loop(0, HEADS, own, 0)
    arrive((1, 1), (7, 1))

    remote(
        pcode.at[pl.ds(1, PLANE - 1)], pcode.at[pl.ds(1, PLANE - 1)], pc_send, pc_recv, in_plane(1)
    ).wait_recv()
    p_to_smem = pltpu.make_async_copy(pcode, rsm, sm_sem.at[1])
    p_to_smem.start()
    p_to_smem.wait()
    for v in range(KV):
        key_copy(v).wait()

    units(0, 0, 1)
    arrive((2, 0), (6, 0))
    arrive((2, 1), (6, 1))
    units(1, 7, 2)
    arrive((3, 0), (5, 0))
    arrive((3, 1), (5, 1))
    units(2, 6, 2)
    arrive((4, 0), (4, 1))
    units(3, 5, 2)

    def back_now(k, i):
        def start():
            level_copy(4, k).start()
            back_copy(4, 0, k).start()
            back_copy(4, 1, k).start()

        if i == 0:
            pl.when(k > 0)(start)
        else:
            start()

    units(4, 4, 1, back_now)

    def pick(s, h, t):
        owner = zsm[s, 0, OWNERS + h * TOPK + t]
        dx = lax.rem(lax.rem(owner, NX) - x + NX, NX)
        dy = lax.rem(lax.div(owner, NX * NZ) - y + NY, NY)
        dz = lax.rem(lax.rem(lax.div(owner, NX), NZ) - z + NZ, NZ)
        away = lax.div(dz + NZ - 1, NZ)
        return away, (dx + NX * dy) * (1 - away)

    def gather_levels(s):
        remote(
            rl[s].at[pl.ds(1, PLANE - 1)], rl[s].at[pl.ds(1, PLANE - 1)],
            ls_send.at[s], ls_recv.at[s], in_plane(1),
        ).wait_recv()

        def body(h, _):
            for t in range(TOPK):
                away, k = pick(s, h, t)
                lt[s, t, pl.ds(h, 1), :] = rl[s][k + PLANE * away]
            return 0

        lax.fori_loop(0, HEADS, body, 0)

    def weigh(c, levels):
        top = functools.reduce(jnp.maximum, levels)
        parts = [jnp.exp(level - top) for level in levels]
        total = functools.reduce(jnp.add, parts)
        inverse = 1.0 / total
        for i, part in enumerate(parts):
            wt[c, i] = part * inverse
        return top + jnp.log(total)

    def picked_levels(s, c):
        return [lt[s, t, :, c * HALF : (c + 1) * HALF] for t in range(TOPK)]

    def picked_sum(s, c, h):
        total = None
        for t in range(TOPK):
            _, k = pick(s, h, t)
            term = wt[c, t, pl.ds(h, 1), :] * ret[s][c][k].astype(jnp.float32)
            total = term if total is None else total + term
        return total

    def wait_back(s, c):
        remote(
            ret[s][c].at[pl.ds(1, PLANE - 1)], ret[s][c].at[pl.ds(1, PLANE - 1)],
            rs_send.at[s], rs_recv.at[s, c], in_plane(1),
        ).wait_recv()

    def wait_sum(s, c):
        remote(
            zacc.at[s, c], zacc.at[s, c], za_send.at[0, c], za_recv.at[s, c], along_z(1)
        ).wait_recv()
        remote(
            zl.at[s, c], zl.at[s, c], zl_send.at[0, c], zl_recv.at[s, c], along_z(1)
        ).wait_recv()

    def sum_copies(s, c):
        down = s < NZ // 2 or (s == NZ // 2 and c == 0)
        to, step = (s - 1, -1) if down else (s + 1, 1)
        return [
            remote(
                zacc.at[s, c], zacc.at[to, c], za_send.at[s, c], za_recv.at[to, c], along_z(step)
            ),
            remote(zl.at[s, c], zl.at[to, c], zl_send.at[s, c], zl_recv.at[to, c], along_z(step)),
        ]

    def combine(s, c):
        upstream = s != NZ // 2 and (s, c) not in ((NZ // 2 - 1, 1), (NZ // 2 + 1, 0))
        wait_back(s, c)
        levels = picked_levels(s, c)
        if upstream:
            wait_sum(s, c)
            levels.append(zl[s, c])
        zl[s, c] = weigh(c, levels)

        def body(h, _):
            total = picked_sum(s, c, h)
            if upstream:
                total += wt[c, TOPK, pl.ds(h, 1), :] * zacc[s, c, h].astype(jnp.float32)
            zacc[s, c, h] = total.astype(jnp.bfloat16)
            return 0

        lax.fori_loop(0, HEADS, body, 0)
        for copy in sum_copies(s, c):
            copy.start()

    for s, c in ((5, 0), (3, 1), (5, 1), (3, 0)):
        send_back(s, c, (s, c) in ((5, 0), (3, 1)))
    gather_levels(4)
    combine(4, 0)
    combine(4, 1)
    for up, down in ((5, 3), (6, 2), (7, 1)):
        if up < 7:
            for s, c in ((up + 1, 0), (down - 1, 1), (up + 1, 1), (down - 1, 0)):
                send_back(s, c, (s, c) in ((up + 1, 0), (down - 1, 1)))
        else:
            send_back(0, 0, True)
            send_back(0, 1, False)
        gather_levels(up)
        combine(up, 0)
        gather_levels(down)
        combine(down, 1)
        combine(up, 1)
        combine(down, 0)

    gather_levels(0)
    for c in range(2):
        wait_back(0, c)
        wait_sum(0, c)
        wait_sum(NZ, c)
        weigh(c, picked_levels(0, c) + [zl[0, c], zl[NZ, c], own_l[c]])

        def finish(h, _, c=c):
            total = picked_sum(0, c, h)
            total += wt[c, TOPK, pl.ds(h, 1), :] * zacc[0, c, h].astype(jnp.float32)
            total += wt[c, TOPK + 1, pl.ds(h, 1), :] * zacc[NZ, c, h].astype(jnp.float32)
            total += wt[c, TOPK + 2, pl.ds(h, 1), :] * own_o[c, h]
            lanes = pl.ds(pl.multiple_of(h * HEAD_SIZE, HEAD_SIZE), HEAD_SIZE)
            out_ref[c * HALF : (c + 1) * HALF, lanes] = total.T.astype(jnp.bfloat16)
            return 0

        lax.fori_loop(0, HEADS, finish, 0)

    z_codes.wait_send()
    remote(
        pcode.at[pl.ds(1, PLANE - 1)], pcode.at[pl.ds(1, PLANE - 1)], pc_send, pc_recv, in_plane(1)
    ).wait_send()
    for copy in pair:
        copy.wait_send()
    half = NZ // 2
    for c in range(2):
        for s in range(NZ):
            if s < half - 1 or (s == half - 1 and c == 0):
                z_query(s, c, s + 1, 1).wait_send()
            if s == 0 or s > half + 1 or (s == half + 1 and c == 1):
                z_query(s, c, (s - 1) % NZ, -1).wait_send()
            if s > 0:
                for copy in sum_copies(s, c):
                    copy.wait_send()
    others = pl.ds(1, PLANE - 1)
    for s in range(NZ):
        remote(
            tx.at[s, :, others], rx.at[s, :, others], tx_send.at[s], rx_recv.at[s, 0, 0], in_plane(1)
        ).wait_send()
        remote(
            rx.at[s, :, others], tx.at[s, :, others], rs_send.at[s], rs_recv.at[s, 0], in_plane(1)
        ).wait_send()
        remote(
            lout.at[s, others], rl[s].at[others], ls_send.at[s], ls_recv.at[s], in_plane(1)
        ).wait_send()


def exchange(q, ck, cv, kp, vp, code):
    dma = pltpu.SemaphoreType.DMA
    bf16, f32 = jnp.bfloat16, jnp.float32
    half = (HEADS, HEAD_SIZE, HALF)
    scratch = [pltpu.VMEM(half, bf16)] * (2 * NZ)
    scratch += [pltpu.VMEM((PLANE, HEAD_SIZE, HALF), bf16)] * (2 * NZ)
    scratch += [pltpu.VMEM((PLANE + 1, 1, ROWS), f32)] * NZ
    scratch += [
        pltpu.VMEM((KV * OWNED, KEY_BLOCK_SIZE, HEAD_SIZE), bf16),
        pltpu.VMEM((2, OWNED, KEY_BLOCK_SIZE, HEAD_SIZE), bf16),
        pltpu.VMEM((KV * OWNED, HEAD_SIZE, KEY_BLOCK_SIZE), bf16),
        pltpu.VMEM((NZ, 2, PLANE, HEAD_SIZE, HALF), bf16),
        pltpu.VMEM((NZ, 2, PLANE, HEAD_SIZE, HALF), bf16),
        pltpu.VMEM((NZ, PLANE, 1, ROWS), f32),
        pltpu.VMEM((NZ + 1, 2) + half, bf16),
        pltpu.VMEM((NZ + 1, 2, HEADS, HALF), f32),
        pltpu.VMEM((2,) + half, f32),
        pltpu.VMEM((2, HEADS, HALF), f32),
        pltpu.VMEM((ROWS, KV * HEAD_SIZE), bf16),
        pltpu.VMEM((KV, HEAD_SIZE, ROWS), bf16),
        pltpu.VMEM((KV, HEAD_SIZE, ROWS), bf16),
        pltpu.VMEM((NZ, TOPK, HEADS, ROWS), f32),
        pltpu.VMEM((2, TOPK + 3, HEADS, HALF), f32),
        pltpu.VMEM((NZ, 1, 2 * OWNERS), jnp.int32),
        pltpu.VMEM((PLANE, NZ, 1, OWNERS), jnp.int32),
        pltpu.SMEM((NZ, 1, 2 * OWNERS), jnp.int32),
        pltpu.SMEM((PLANE, NZ, 1, OWNERS), jnp.int32),
        dma((KV,)), dma((KV,)),
        dma((2, NZ, 2)), dma((NZ, 2)),
        dma, dma, dma, dma, dma((2,)),
        dma((2,)), dma((2,)),
        dma((NZ,)), dma((NZ, 2, PLANE)),
        dma((NZ,)), dma((NZ, 2)),
        dma((NZ,)), dma((NZ,)),
        dma((NZ, 2)), dma((NZ + 1, 2)), dma((NZ, 2)), dma((NZ + 1, 2)),
    ]
    vmem = pl.BlockSpec(memory_space=pltpu.VMEM)
    hbm = pl.BlockSpec(memory_space=pl.ANY)
    return pl.pallas_call(
        kernel,
        out_shape=jax.ShapeDtypeStruct((ROWS, HEADS * HEAD_SIZE), bf16),
        in_specs=[vmem, vmem, vmem, hbm, hbm, vmem],
        out_specs=vmem,
        scratch_shapes=scratch,
        compiler_params=pltpu.CompilerParams(
            collective_id=0, has_side_effects=True, vmem_limit_bytes=62 << 20
        ),
        name="attend",
    )(q, ck, cv, kp, vp, code)


def local(queries, current_keys, current_values, cached_key_pages, cached_value_pages, picks):
    chosen = picks.reshape(HEADS * TOPK)
    owner = chosen // OWNED
    head = jnp.arange(HEADS * TOPK) // TOPK
    table = head // GROUP * OWNED + chosen % OWNED
    value = head + HEADS * table
    by_owner = jnp.sum(
        jnp.where(owner[None, :] == jnp.arange(OWNERS)[:, None], value[None, :], 0), axis=1
    )
    code = jnp.concatenate([by_owner, jnp.pad(owner, (0, OWNERS - HEADS * TOPK))])
    return exchange(
        queries,
        current_keys,
        current_values,
        cached_key_pages.reshape(OWNED, KEY_BLOCK_SIZE, KV * HEAD_SIZE),
        cached_value_pages.reshape(OWNED, KEY_BLOCK_SIZE, KV * HEAD_SIZE),
        code.reshape(1, 2 * OWNERS).astype(jnp.int32),
    )


def solution(mesh):
    placed = (
        P("ctx", "kvh"),
        P("ctx", "kvh"),
        P("ctx", "kvh"),
        P("ctx", "kvh"),
        P("ctx", "kvh"),
        P("ctx", "kvh", None),
    )
    return jax.shard_map(
        local, mesh=mesh, in_specs=placed, out_specs=P("ctx", "kvh"), check_vma=False
    )
```

```python
import functools

import jax
import jax.numpy as jnp
from jax import lax
from jax.experimental import pallas as pl
from jax.experimental.pallas import tpu as pltpu
from jax.sharding import PartitionSpec as P

HEAD_SIZE = 128
KEY_BLOCK_SIZE = 512
TOPK = 3
MESH = pl.DeviceIdType.MESH
NX, NY, NZ = 4, 4, 8
PLANE = NX * NY
HEADS = 16
KV = 4
GROUP = HEADS // KV
OWNED = 8
ROWS = 256
HALF = 128
OWNERS = 128
SCALE = HEAD_SIZE**-0.5
SCALE2 = SCALE * 1.4426950408889634
LOW = -1e30


def kernel(*refs):
    (q_ref, ck_ref, cv_ref, kp_ref, vp_ref, code_ref, csm, out_ref), refs = refs[:8], refs[8:]
    zq, refs = [refs[2 * s : 2 * s + 2] for s in range(NZ)], refs[2 * NZ :]
    ret, refs = [refs[2 * s : 2 * s + 2] for s in range(NZ)], refs[2 * NZ :]
    rl, refs = refs[:NZ], refs[NZ:]
    (
        kbuf, vstage, vbuf, tx, rx, lout, zacc, zl, own_o, own_l, pk, pvt, cvt, lt, wt,
        zcode, pcode, zsm, rsm,
        k_sem, v_sem, zq_send, zq_recv, zc_send, zc_recv, pc_send, pc_recv, sm_sem,
        xp_send, xp_recv, tx_send, rx_recv, rs_send, rs_recv, ls_send, ls_recv,
        za_send, za_recv, zl_send, zl_recv,
    ) = refs
    me = lax.axis_index("ctx")
    core = lax.axis_index("kvh")
    x = lax.rem(me, NX)
    z = lax.rem(me // NX, NZ)
    y = me // (NX * NZ)

    def in_plane(k):
        return (
            lax.rem(y + k // NX, NY) * (NX * NZ) + z * NX + lax.rem(x + lax.rem(k, NX), NX),
            core,
        )

    def opposite(k):
        return (
            lax.rem(y + NY - k // NX, NY) * (NX * NZ)
            + z * NX
            + lax.rem(x + NX - lax.rem(k, NX), NX),
            core,
        )

    def along_z(d):
        return (y * (NX * NZ) + lax.rem(z + d + NZ, NZ) * NX + x, core)

    def owner_at(k):
        return in_plane(k)[0]

    def remote(src, dst, send, recv, device):
        return pltpu.make_async_remote_copy(
            src_ref=src,
            dst_ref=dst,
            send_sem=send,
            recv_sem=recv,
            device_id=device,
            device_id_type=MESH,
        )

    def key_copy(v):
        return pltpu.make_async_copy(
            kp_ref.at[:, :, pl.ds(v * HEAD_SIZE, HEAD_SIZE)],
            kbuf.at[pl.ds(v * OWNED, OWNED)],
            k_sem.at[v],
        )

    def value_copy(v):
        return pltpu.make_async_copy(
            vp_ref.at[:, :, pl.ds(v * HEAD_SIZE, HEAD_SIZE)], vstage.at[v % 2], v_sem.at[v]
        )

    value_copy(0).start()
    value_copy(1).start()
    for v in range(KV):
        key_copy(v).start()

    barrier = pltpu.get_barrier_semaphore()
    for k in range(1, PLANE):
        pl.semaphore_signal(barrier, inc=1, device_id=in_plane(k), device_id_type=MESH)
    for d in range(1, NZ):
        pl.semaphore_signal(barrier, inc=1, device_id=along_z(d), device_id_type=MESH)

    for c in range(2):
        for h in range(HEADS):
            zq[0][c][h] = q_ref[
                c * HALF : (c + 1) * HALF, h * HEAD_SIZE : (h + 1) * HEAD_SIZE
            ].T
    for v in range(KV):
        cvt[v] = cv_ref[:, v * HEAD_SIZE : (v + 1) * HEAD_SIZE].T
    zcode[0] = code_ref[...]
    pl.semaphore_wait(barrier, PLANE - 1 + NZ - 1)

    def z_query(s, c, step):
        to = (s + step) % NZ
        heads = pl.ds(0, HEADS)
        if to == NZ // 2:
            heads = pl.ds(0 if step > 0 else HEADS // 2, HEADS // 2)
        return remote(
            zq[s][c].at[heads],
            zq[to][c].at[heads],
            zq_send.at[0 if step > 0 else 1, s, c],
            zq_recv.at[NZ if to == NZ // 2 and step < 0 else to, c],
            along_z(step),
        )

    for c in range(2):
        z_query(0, c, 1).start()
        z_query(0, c, -1).start()

    def z_code(d):
        return remote(zcode.at[0], zcode.at[d], zc_send, zc_recv, along_z(d))

    for d in range(1, NZ):
        z_code(d).start()

    z_codes = remote(
        zcode.at[pl.ds(1, NZ - 1)], zcode.at[pl.ds(1, NZ - 1)], zc_send, zc_recv, along_z(1)
    )
    def query_copy(s, c, k):
        return remote(
            tx.at[s, c, k], rx.at[s, c, k], tx_send.at[s], rx_recv.at[s, c, k], in_plane(k)
        )

    def send_out(s, c):
        def head_for(k):
            owner = owner_at(k)
            return lax.rem(csm[0, owner] if s == 0 else zsm[s, 0, owner], HEADS)

        rx[s, c, 0] = zq[s][c][head_for(0)]

        def body(k, _):
            tx[s, c, k] = zq[s][c][head_for(k)]
            query_copy(s, c, k).start()
            return 0

        lax.fori_loop(1, PLANE, body, 0)

    def pass_on(s, c):
        for step in (1, -1):
            if s == NZ // 2 or (s < NZ // 2) == (step > 0):
                z_query((s - step) % NZ, c, step).wait_recv()
                if s != NZ // 2:
                    z_query(s, c, step).start()

    def arrive(*pairs):
        for s, c in pairs:
            pass_on(s, c)
        for s, c in pairs:
            send_out(s, c)

    def attend(keys, queries, values):
        scores = jnp.dot(keys, queries, preferred_element_type=jnp.float32)
        top = jnp.max(scores, axis=0, keepdims=True)
        weights = jnp.exp2(scores * SCALE2 - top * SCALE2)
        total = jnp.sum(weights, axis=0, keepdims=True)
        out = jnp.dot(values, weights.astype(jnp.bfloat16), preferred_element_type=jnp.float32)
        return out * (1.0 / total), top * SCALE + jnp.log(total)

    def unit(s, k):
        table = lax.div(rsm[k, s, 0, me], HEADS)
        queries = jnp.concatenate([rx[s, 0, k], rx[s, 1, k]], axis=1)
        out, level = attend(kbuf[table], queries, vbuf[table])
        out = out.astype(jnp.bfloat16)
        rx[s, 0, k] = out[:, :HALF]
        rx[s, 1, k] = out[:, HALF:]
        lout[s, k] = level

    def back_copy(s, c, k):
        return remote(
            rx.at[s, c, k], ret[s][c].at[k], rs_send.at[s], rs_recv.at[s, c], opposite(k)
        )

    def level_copy(s, k):
        return remote(lout.at[s, k], rl[s].at[k], ls_send.at[s], ls_recv.at[s], opposite(k))

    def units(a, b, count, then=None):
        def body(j, _):
            s = a + (b - a) * lax.div(j, PLANE // 2)
            for i in range(2):
                k = lax.rem(j, PLANE // 2) * 2 + i

                def wait(k=k):
                    query_copy(s, 0, k).wait_recv()
                    query_copy(s, 1, k).wait_recv()

                if i == 0:
                    pl.when(k > 0)(wait)
                else:
                    wait()
            for i in range(2):
                unit(s, lax.rem(j, PLANE // 2) * 2 + i)
            if then is not None:
                for i in range(2):
                    then(lax.rem(j, PLANE // 2) * 2 + i, i)
            return 0

        lax.fori_loop(0, count * PLANE // 2, body, 0)
        for s in (a, b)[:count]:
            for c in range(2):
                ret[s][c][0] = rx[s, c, 0]
            rl[s][0] = lout[s, 0]
            rl[s][PLANE] = jnp.full((1, ROWS), LOW, jnp.float32)

    def send_back(s, c, with_level):
        def body(k, _):
            back_copy(s, c, k).start()
            if with_level:
                level_copy(s, k).start()
            return 0

        lax.fori_loop(1, PLANE, body, 0)

    send_out(0, 0)
    send_out(0, 1)
    odd = lax.rem(me, 2)
    partner = (me + 1 - 2 * odd, core)
    pair = [
        remote(ck_ref, pk, xp_send.at[0], xp_recv.at[0], partner),
        remote(cvt, pvt, xp_send.at[1], xp_recv.at[1], partner),
    ]
    for copy in pair:
        copy.start()

    for v in range(KV):
        value_copy(v).wait()

        def turn(w, _, v=v):
            vbuf[v * OWNED + w] = vstage[v % 2, w].T
            return 0

        lax.fori_loop(0, OWNED, turn, 0)
        if v + 2 < KV:
            value_copy(v + 2).start()

    z_codes.wait_recv()

    def p_code(k):
        return remote(
            zcode.at[:, :, pl.ds(0, OWNERS)], pcode.at[k], pc_send, pc_recv, in_plane(k)
        )

    def start_p_code(k, _):
        p_code(k).start()
        return 0

    lax.fori_loop(1, PLANE, start_p_code, 0)
    pcode[0] = zcode[:, :, :OWNERS]
    z_to_smem = pltpu.make_async_copy(zcode, zsm, sm_sem.at[0])
    z_to_smem.start()
    z_to_smem.wait()

    arrive((1, 0), (7, 0))

    for copy in pair:
        copy.wait_recv()

    def own(h, _):
        v = h // GROUP
        lanes = pl.ds(pl.multiple_of(v * HEAD_SIZE, HEAD_SIZE), HEAD_SIZE)
        queries = jnp.concatenate([zq[0][0][h], zq[0][1][h]], axis=1)
        before = jnp.dot(pk[:, lanes], queries, preferred_element_type=jnp.float32)
        here = jnp.dot(ck_ref[:, lanes], queries, preferred_element_type=jnp.float32)
        key_pos = lax.broadcasted_iota(jnp.int32, (ROWS, ROWS), 0)
        query_pos = lax.broadcasted_iota(jnp.int32, (ROWS, ROWS), 1)
        before = jnp.where(odd == 1, before, LOW)
        here = jnp.where(key_pos <= query_pos, here, LOW)
        top = jnp.maximum(
            jnp.max(before, axis=0, keepdims=True), jnp.max(here, axis=0, keepdims=True)
        )
        weights_before = jnp.exp2((before - top) * SCALE2)
        weights_here = jnp.exp2((here - top) * SCALE2)
        total = jnp.sum(weights_before, axis=0, keepdims=True) + jnp.sum(
            weights_here, axis=0, keepdims=True
        )
        out = jnp.dot(pvt[v], weights_before.astype(jnp.bfloat16), preferred_element_type=jnp.float32)
        out += jnp.dot(cvt[v], weights_here.astype(jnp.bfloat16), preferred_element_type=jnp.float32)
        out = out * (1.0 / total)
        level = top * SCALE + jnp.log(total)
        for c in range(2):
            own_o[c, h] = out[:, c * HALF : (c + 1) * HALF]
            own_l[c, pl.ds(h, 1), :] = level[:, c * HALF : (c + 1) * HALF]
        return 0

    lax.fori_loop(0, HEADS, own, 0)
    arrive((1, 1), (7, 1))

    remote(
        pcode.at[pl.ds(1, PLANE - 1)], pcode.at[pl.ds(1, PLANE - 1)], pc_send, pc_recv, in_plane(1)
    ).wait_recv()
    p_to_smem = pltpu.make_async_copy(pcode, rsm, sm_sem.at[1])
    p_to_smem.start()
    p_to_smem.wait()
    for v in range(KV):
        key_copy(v).wait()

    units(0, 0, 1)
    arrive((2, 0), (6, 0))
    arrive((2, 1), (6, 1))
    units(1, 7, 2)
    arrive((3, 0), (5, 0))
    arrive((3, 1), (5, 1))
    units(2, 6, 2)
    arrive((4, 0), (4, 1))
    units(3, 5, 2)

    def back_now(k, i):
        def start():
            level_copy(4, k).start()
            back_copy(4, 0, k).start()
            back_copy(4, 1, k).start()

        if i == 0:
            pl.when(k > 0)(start)
        else:
            start()

    send_back(0, 0, True)
    send_back(0, 1, False)
    units(4, 4, 1, back_now)

    def pick(s, h, t):
        owner = zsm[s, 0, OWNERS + h * TOPK + t]
        dx = lax.rem(lax.rem(owner, NX) - x + NX, NX)
        dy = lax.rem(lax.div(owner, NX * NZ) - y + NY, NY)
        dz = lax.rem(lax.rem(lax.div(owner, NX), NZ) - z + NZ, NZ)
        away = lax.div(dz + NZ - 1, NZ)
        return away, (dx + NX * dy) * (1 - away)

    def gather_levels(s):
        remote(
            rl[s].at[pl.ds(1, PLANE - 1)], rl[s].at[pl.ds(1, PLANE - 1)],
            ls_send.at[s], ls_recv.at[s], in_plane(1),
        ).wait_recv()

        def body(h, _):
            for t in range(TOPK):
                away, k = pick(s, h, t)
                lt[s, t, pl.ds(h, 1), :] = rl[s][k + PLANE * away]
            return 0

        lax.fori_loop(0, HEADS, body, 0)

    def weigh(c, heads, levels):
        top = functools.reduce(jnp.maximum, levels)
        parts = [jnp.exp(level - top) for level in levels]
        total = functools.reduce(jnp.add, parts)
        inverse = 1.0 / total
        for i, part in enumerate(parts):
            wt[c, i, heads] = part * inverse
        return top + jnp.log(total)

    def picked_levels(s, c, heads):
        return [lt[s, t, heads, c * HALF : (c + 1) * HALF] for t in range(TOPK)]

    def picked_sum(s, c, h):
        total = None
        for t in range(TOPK):
            _, k = pick(s, h, t)
            term = wt[c, t, pl.ds(h, 1), :] * ret[s][c][k].astype(jnp.float32)
            total = term if total is None else total + term
        return total

    def wait_back(s, c):
        remote(
            ret[s][c].at[pl.ds(1, PLANE - 1)], ret[s][c].at[pl.ds(1, PLANE - 1)],
            rs_send.at[s], rs_recv.at[s, c], in_plane(1),
        ).wait_recv()

    def sum_copies(s, c, step):
        to = s + step
        heads = pl.ds(0, HEADS)
        if s == NZ // 2:
            heads = pl.ds(0 if step > 0 else HEADS // 2, HEADS // 2)
        way = 0 if step > 0 else 1
        return [
            remote(
                zacc.at[s, c, heads], zacc.at[to, c, heads], za_send.at[way, s, c],
                za_recv.at[to, c], along_z(step),
            ),
            remote(
                zl.at[s, c, heads], zl.at[to, c, heads], zl_send.at[way, s, c],
                zl_recv.at[to, c], along_z(step),
            ),
        ]

    def steps_from(s):
        return (1, -1) if s == NZ // 2 else (-1,) if s < NZ // 2 else (1,)

    def wait_sum(s, c, step):
        for copy in sum_copies(s - step, c, step):
            copy.wait_recv()

    def combine(s, c):
        wait_back(s, c)
        half = HEADS // 2
        if s == NZ // 2:
            parts = [(0, HEADS, False)]
        elif s == NZ // 2 + 1:
            parts = [(half, half, False), (0, half, True)]
        elif s == NZ // 2 - 1:
            parts = [(0, half, False), (half, half, True)]
        else:
            parts = [(0, HEADS, True)]
        for start, count, upstream in parts:
            heads = slice(start, start + count)
            levels = picked_levels(s, c, heads)
            if upstream:
                wait_sum(s, c, 1 if s > NZ // 2 else -1)
                levels.append(zl[s, c, heads])
            zl[s, c, heads] = weigh(c, heads, levels)

            def body(h, _, upstream=upstream):
                total = picked_sum(s, c, h)
                if upstream:
                    total += wt[c, TOPK, pl.ds(h, 1), :] * zacc[s, c, h].astype(jnp.float32)
                zacc[s, c, h] = total.astype(jnp.bfloat16)
                return 0

            lax.fori_loop(start, start + count, body, 0)
        for step in steps_from(s):
            for copy in sum_copies(s, c, step):
                copy.start()

    for c in range(2):
        send_back(5, c, c == 0)
        send_back(3, c, c == 0)
    gather_levels(4)
    combine(4, 0)
    combine(4, 1)
    for up, down in ((5, 3), (6, 2), (7, 1)):
        if up < 7:
            for c in range(2):
                send_back(up + 1, c, c == 0)
                send_back(down - 1, c, c == 0)
        gather_levels(up)
        gather_levels(down)
        for c in range(2):
            combine(up, c)
            combine(down, c)

    gather_levels(0)
    for c in range(2):
        wait_back(0, c)
        wait_sum(0, c, -1)
        wait_sum(NZ, c, 1)
        every = slice(0, HEADS)
        weigh(c, every, picked_levels(0, c, every) + [zl[0, c], zl[NZ, c], own_l[c]])

        def finish(h, _, c=c):
            total = picked_sum(0, c, h)
            total += wt[c, TOPK, pl.ds(h, 1), :] * zacc[0, c, h].astype(jnp.float32)
            total += wt[c, TOPK + 1, pl.ds(h, 1), :] * zacc[NZ, c, h].astype(jnp.float32)
            total += wt[c, TOPK + 2, pl.ds(h, 1), :] * own_o[c, h]
            lanes = pl.ds(pl.multiple_of(h * HEAD_SIZE, HEAD_SIZE), HEAD_SIZE)
            out_ref[c * HALF : (c + 1) * HALF, lanes] = total.T.astype(jnp.bfloat16)
            return 0

        lax.fori_loop(0, HEADS, finish, 0)

    z_codes.wait_send()
    remote(
        pcode.at[pl.ds(1, PLANE - 1)], pcode.at[pl.ds(1, PLANE - 1)], pc_send, pc_recv, in_plane(1)
    ).wait_send()
    for copy in pair:
        copy.wait_send()
    for c in range(2):
        for s in range(NZ):
            for step in (1, -1):
                if s == 0 or (s != NZ // 2 and (s < NZ // 2) == (step > 0)):
                    z_query(s, c, step).wait_send()
            if s > 0:
                for step in steps_from(s):
                    for copy in sum_copies(s, c, step):
                        copy.wait_send()
    others = pl.ds(1, PLANE - 1)
    for s in range(NZ):
        remote(
            tx.at[s, :, others], rx.at[s, :, others], tx_send.at[s], rx_recv.at[s, 0, 0], in_plane(1)
        ).wait_send()
        remote(
            rx.at[s, :, others], tx.at[s, :, others], rs_send.at[s], rs_recv.at[s, 0], in_plane(1)
        ).wait_send()
        remote(
            lout.at[s, others], rl[s].at[others], ls_send.at[s], ls_recv.at[s], in_plane(1)
        ).wait_send()


def exchange(q, ck, cv, kp, vp, code):
    dma = pltpu.SemaphoreType.DMA
    bf16, f32 = jnp.bfloat16, jnp.float32
    half = (HEADS, HEAD_SIZE, HALF)
    scratch = [pltpu.VMEM(half, bf16)] * (2 * NZ)
    scratch += [pltpu.VMEM((PLANE, HEAD_SIZE, HALF), bf16)] * (2 * NZ)
    scratch += [pltpu.VMEM((PLANE + 1, 1, ROWS), f32)] * NZ
    scratch += [
        pltpu.VMEM((KV * OWNED, KEY_BLOCK_SIZE, HEAD_SIZE), bf16),
        pltpu.VMEM((2, OWNED, KEY_BLOCK_SIZE, HEAD_SIZE), bf16),
        pltpu.VMEM((KV * OWNED, HEAD_SIZE, KEY_BLOCK_SIZE), bf16),
        pltpu.VMEM((NZ, 2, PLANE, HEAD_SIZE, HALF), bf16),
        pltpu.VMEM((NZ, 2, PLANE, HEAD_SIZE, HALF), bf16),
        pltpu.VMEM((NZ, PLANE, 1, ROWS), f32),
        pltpu.VMEM((NZ + 1, 2) + half, bf16),
        pltpu.VMEM((NZ + 1, 2, HEADS, HALF), f32),
        pltpu.VMEM((2,) + half, f32),
        pltpu.VMEM((2, HEADS, HALF), f32),
        pltpu.VMEM((ROWS, KV * HEAD_SIZE), bf16),
        pltpu.VMEM((KV, HEAD_SIZE, ROWS), bf16),
        pltpu.VMEM((KV, HEAD_SIZE, ROWS), bf16),
        pltpu.VMEM((NZ, TOPK, HEADS, ROWS), f32),
        pltpu.VMEM((2, TOPK + 3, HEADS, HALF), f32),
        pltpu.VMEM((NZ, 1, 2 * OWNERS), jnp.int32),
        pltpu.VMEM((PLANE, NZ, 1, OWNERS), jnp.int32),
        pltpu.SMEM((NZ, 1, 2 * OWNERS), jnp.int32),
        pltpu.SMEM((PLANE, NZ, 1, OWNERS), jnp.int32),
        dma((KV,)), dma((KV,)),
        dma((2, NZ, 2)), dma((NZ + 1, 2)),
        dma, dma, dma, dma, dma((2,)),
        dma((2,)), dma((2,)),
        dma((NZ,)), dma((NZ, 2, PLANE)),
        dma((NZ,)), dma((NZ, 2)),
        dma((NZ,)), dma((NZ,)),
        dma((2, NZ, 2)), dma((NZ + 1, 2)), dma((2, NZ, 2)), dma((NZ + 1, 2)),
    ]
    vmem = pl.BlockSpec(memory_space=pltpu.VMEM)
    hbm = pl.BlockSpec(memory_space=pl.ANY)
    return pl.pallas_call(
        kernel,
        out_shape=jax.ShapeDtypeStruct((ROWS, HEADS * HEAD_SIZE), bf16),
        in_specs=[vmem, vmem, vmem, hbm, hbm, vmem, pl.BlockSpec(memory_space=pltpu.SMEM)],
        out_specs=vmem,
        scratch_shapes=scratch,
        compiler_params=pltpu.CompilerParams(
            collective_id=0, has_side_effects=True, vmem_limit_bytes=62 << 20
        ),
        name="attend",
    )(q, ck, cv, kp, vp, code, code)


def local(queries, current_keys, current_values, cached_key_pages, cached_value_pages, picks):
    chosen = picks.reshape(HEADS * TOPK)
    owner = chosen // OWNED
    head = jnp.arange(HEADS * TOPK) // TOPK
    table = head // GROUP * OWNED + chosen % OWNED
    value = head + HEADS * table
    by_owner = jnp.sum(
        jnp.where(owner[None, :] == jnp.arange(OWNERS)[:, None], value[None, :], 0), axis=1
    )
    code = jnp.concatenate([by_owner, jnp.pad(owner, (0, OWNERS - HEADS * TOPK))])
    return exchange(
        queries,
        current_keys,
        current_values,
        cached_key_pages.reshape(OWNED, KEY_BLOCK_SIZE, KV * HEAD_SIZE),
        cached_value_pages.reshape(OWNED, KEY_BLOCK_SIZE, KV * HEAD_SIZE),
        code.reshape(1, 2 * OWNERS).astype(jnp.int32),
    )


def solution(mesh):
    placed = (
        P("ctx", "kvh"),
        P("ctx", "kvh"),
        P("ctx", "kvh"),
        P("ctx", "kvh"),
        P("ctx", "kvh"),
        P("ctx", "kvh", None),
    )
    return jax.shard_map(
        local, mesh=mesh, in_specs=placed, out_specs=P("ctx", "kvh"), check_vma=False
    )
```

```python
import functools

import jax
import jax.numpy as jnp
from jax import lax
from jax.experimental import pallas as pl
from jax.experimental.pallas import tpu as pltpu
from jax.sharding import PartitionSpec as P

HEAD_SIZE = 128
KEY_BLOCK_SIZE = 512
TOPK = 3
MESH = pl.DeviceIdType.MESH
NX, NY, NZ = 4, 4, 8
PLANE = NX * NY
HEADS = 16
KV = 4
GROUP = HEADS // KV
OWNED = 8
ROWS = 256
HALF = 128
OWNERS = 128
SCALE = HEAD_SIZE**-0.5
SCALE2 = SCALE * 1.4426950408889634
LOW = -1e30


def kernel(*refs):
    (q_ref, ck_ref, cv_ref, kp_ref, vp_ref, code_ref, csm, out_ref), refs = refs[:8], refs[8:]
    zq, refs = [refs[2 * s : 2 * s + 2] for s in range(NZ)], refs[2 * NZ :]
    ret, refs = [refs[2 * s : 2 * s + 2] for s in range(NZ)], refs[2 * NZ :]
    rl, refs = [refs[2 * s : 2 * s + 2] for s in range(NZ)], refs[2 * NZ :]
    (
        kbuf, vstage, vbuf, tx, rx, lout, zacc, zl, own_o, own_l, pk, pvt, cvt, lt, wt,
        zcode, pcode, zsm, rsm,
        k_sem, v_sem, zq_send, zq_recv, zc_send, zc_recv, pc_send, pc_recv, sm_sem,
        xp_send, xp_recv, tx_send, rx_recv, rs_send, rs_recv, ls_send, ls_recv,
        za_send, za_recv, zl_send, zl_recv,
    ) = refs
    me = lax.axis_index("ctx")
    core = lax.axis_index("kvh")
    x = lax.rem(me, NX)
    z = lax.rem(me // NX, NZ)
    y = me // (NX * NZ)

    def in_plane(k):
        return (
            lax.rem(y + k // NX, NY) * (NX * NZ) + z * NX + lax.rem(x + lax.rem(k, NX), NX),
            core,
        )

    def opposite(k):
        return (
            lax.rem(y + NY - k // NX, NY) * (NX * NZ)
            + z * NX
            + lax.rem(x + NX - lax.rem(k, NX), NX),
            core,
        )

    def along_z(d):
        return (y * (NX * NZ) + lax.rem(z + d + NZ, NZ) * NX + x, core)

    def owner_at(k):
        return in_plane(k)[0]

    def remote(src, dst, send, recv, device):
        return pltpu.make_async_remote_copy(
            src_ref=src,
            dst_ref=dst,
            send_sem=send,
            recv_sem=recv,
            device_id=device,
            device_id_type=MESH,
        )

    def key_copy(v):
        return pltpu.make_async_copy(
            kp_ref.at[:, :, pl.ds(v * HEAD_SIZE, HEAD_SIZE)],
            kbuf.at[pl.ds(v * OWNED, OWNED)],
            k_sem.at[v],
        )

    def value_copy(v):
        return pltpu.make_async_copy(
            vp_ref.at[:, :, pl.ds(v * HEAD_SIZE, HEAD_SIZE)], vstage.at[v % 2], v_sem.at[v]
        )

    value_copy(0).start()
    value_copy(1).start()
    for v in range(KV):
        key_copy(v).start()

    barrier = pltpu.get_barrier_semaphore()
    for k in range(1, PLANE):
        pl.semaphore_signal(barrier, inc=1, device_id=in_plane(k), device_id_type=MESH)
    for d in range(1, NZ):
        pl.semaphore_signal(barrier, inc=1, device_id=along_z(d), device_id_type=MESH)

    for c in range(2):
        for h in range(HEADS):
            zq[0][c][h] = q_ref[
                c * HALF : (c + 1) * HALF, h * HEAD_SIZE : (h + 1) * HEAD_SIZE
            ].T
    for v in range(KV):
        cvt[v] = cv_ref[:, v * HEAD_SIZE : (v + 1) * HEAD_SIZE].T
    zcode[0] = code_ref[...]
    pl.semaphore_wait(barrier, PLANE - 1 + NZ - 1)

    def z_query(s, c, step, part):
        to = (s + step) % NZ
        heads = pl.ds(part * (HEADS // 2), HEADS // 2)
        return remote(
            zq[s][c].at[heads],
            zq[to][c].at[heads],
            zq_send.at[0 if step > 0 else 1, s, c, part],
            zq_recv.at[to, c, part],
            along_z(step),
        )

    def parts_to(s, step):
        return (0, 1) if (s + step) % NZ != NZ // 2 else (0,) if step > 0 else (1,)

    def start_ring(c):
        for part in range(2):
            for step in (1, -1):
                z_query(0, c, step, part).start()

    start_ring(0)

    def z_code(d):
        return remote(zcode.at[0], zcode.at[d], zc_send, zc_recv, along_z(d))

    for d in range(1, NZ):
        z_code(d).start()

    z_codes = remote(
        zcode.at[pl.ds(1, NZ - 1)], zcode.at[pl.ds(1, NZ - 1)], zc_send, zc_recv, along_z(1)
    )
    def query_copy(s, c, k):
        return remote(
            tx.at[s, c, k], rx.at[s, c, k], tx_send.at[s], rx_recv.at[s, c, k], in_plane(k)
        )

    def send_out(s, c):
        def head_for(k):
            owner = owner_at(k)
            return lax.rem(csm[0, owner] if s == 0 else zsm[s, 0, owner], HEADS)

        rx[s, c, 0] = zq[s][c][head_for(0)]

        def body(k, _):
            tx[s, c, k] = zq[s][c][head_for(k)]
            query_copy(s, c, k).start()
            return 0

        lax.fori_loop(1, PLANE, body, 0)

    def pass_on(s, c):
        for step in (1, -1):
            if s == NZ // 2 or (s < NZ // 2) == (step > 0):
                for part in parts_to(s - step, step):
                    z_query((s - step) % NZ, c, step, part).wait_recv()
                    if s != NZ // 2 and part in parts_to(s, step):
                        z_query(s, c, step, part).start()

    def arrive(*pairs):
        for s, c in pairs:
            pass_on(s, c)
        for s, c in pairs:
            send_out(s, c)

    def attend(keys, queries, values):
        scores = jnp.dot(keys, queries, preferred_element_type=jnp.float32)
        top = jnp.max(scores, axis=0, keepdims=True)
        weights = jnp.exp2(scores * SCALE2 - top * SCALE2)
        total = jnp.sum(weights, axis=0, keepdims=True)
        out = jnp.dot(values, weights.astype(jnp.bfloat16), preferred_element_type=jnp.float32)
        return out * (1.0 / total), top * SCALE + jnp.log(total)

    def unit(s, c, k):
        table = lax.div(rsm[k, s, 0, me], HEADS)
        out, level = attend(kbuf[table], rx[s, c, k], vbuf[table])
        rx[s, c, k] = out.astype(jnp.bfloat16)
        lout[s, c, k] = level

    def back_copy(s, c, k):
        return remote(
            rx.at[s, c, k], ret[s][c].at[k], rs_send.at[s], rs_recv.at[s, c], opposite(k)
        )

    def level_copy(s, c, k):
        return remote(
            lout.at[s, c, k], rl[s][c].at[k], ls_send.at[s], ls_recv.at[s, c], opposite(k)
        )

    def units(c, a, b, then=False):
        count = 1 if b is None else 2

        def body(j, _):
            s = a if b is None else a + (b - a) * lax.div(j, PLANE // 2)
            for i in range(2):
                k = lax.rem(j, PLANE // 2) * 2 + i

                def wait(k=k):
                    query_copy(s, c, k).wait_recv()

                if i == 0:
                    pl.when(k > 0)(wait)
                else:
                    wait()
            for i in range(2):
                unit(s, c, lax.rem(j, PLANE // 2) * 2 + i)
            for i in range(2 if then else 0):
                k = lax.rem(j, PLANE // 2) * 2 + i

                def start(k=k):
                    level_copy(s, c, k).start()
                    back_copy(s, c, k).start()

                if i == 0:
                    pl.when(k > 0)(start)
                else:
                    start()
            return 0

        lax.fori_loop(0, count * PLANE // 2, body, 0)
        for s in (a, b)[:count]:
            ret[s][c][0] = rx[s, c, 0]
            rl[s][c][0] = lout[s, c, 0]
            rl[s][c][PLANE] = jnp.full((1, HALF), LOW, jnp.float32)

    def send_back(c, *slots):
        for s in slots:

            def body(k, _, s=s):
                level_copy(s, c, k).start()
                back_copy(s, c, k).start()
                return 0

            lax.fori_loop(1, PLANE, body, 0)

    send_out(0, 0)
    send_out(0, 1)
    odd = lax.rem(me, 2)
    partner = (me + 1 - 2 * odd, core)
    pair = [
        remote(ck_ref, pk, xp_send.at[0], xp_recv.at[0], partner),
        remote(cvt, pvt, xp_send.at[1], xp_recv.at[1], partner),
    ]
    for copy in pair:
        copy.start()

    for v in range(KV):
        value_copy(v).wait()

        def turn(w, _, v=v):
            vbuf[v * OWNED + w] = vstage[v % 2, w].T
            return 0

        lax.fori_loop(0, OWNED, turn, 0)
        if v + 2 < KV:
            value_copy(v + 2).start()

    z_codes.wait_recv()

    def p_code(k):
        return remote(
            zcode.at[:, :, pl.ds(0, OWNERS)], pcode.at[k], pc_send, pc_recv, in_plane(k)
        )

    def start_p_code(k, _):
        p_code(k).start()
        return 0

    lax.fori_loop(1, PLANE, start_p_code, 0)
    pcode[0] = zcode[:, :, :OWNERS]
    z_to_smem = pltpu.make_async_copy(zcode, zsm, sm_sem.at[0])
    z_to_smem.start()
    z_to_smem.wait()

    arrive((1, 0), (7, 0))

    for copy in pair:
        copy.wait_recv()

    def own(h, _):
        v = h // GROUP
        lanes = pl.ds(pl.multiple_of(v * HEAD_SIZE, HEAD_SIZE), HEAD_SIZE)
        queries = jnp.concatenate([zq[0][0][h], zq[0][1][h]], axis=1)
        before = jnp.dot(pk[:, lanes], queries, preferred_element_type=jnp.float32)
        here = jnp.dot(ck_ref[:, lanes], queries, preferred_element_type=jnp.float32)
        key_pos = lax.broadcasted_iota(jnp.int32, (ROWS, ROWS), 0)
        query_pos = lax.broadcasted_iota(jnp.int32, (ROWS, ROWS), 1)
        before = jnp.where(odd == 1, before, LOW)
        here = jnp.where(key_pos <= query_pos, here, LOW)
        top = jnp.maximum(
            jnp.max(before, axis=0, keepdims=True), jnp.max(here, axis=0, keepdims=True)
        )
        weights_before = jnp.exp2((before - top) * SCALE2)
        weights_here = jnp.exp2((here - top) * SCALE2)
        total = jnp.sum(weights_before, axis=0, keepdims=True) + jnp.sum(
            weights_here, axis=0, keepdims=True
        )
        out = jnp.dot(pvt[v], weights_before.astype(jnp.bfloat16), preferred_element_type=jnp.float32)
        out += jnp.dot(cvt[v], weights_here.astype(jnp.bfloat16), preferred_element_type=jnp.float32)
        out = out * (1.0 / total)
        level = top * SCALE + jnp.log(total)
        for c in range(2):
            own_o[c, h] = out[:, c * HALF : (c + 1) * HALF]
            own_l[c, pl.ds(h, 1), :] = level[:, c * HALF : (c + 1) * HALF]
        return 0

    lax.fori_loop(0, HEADS, own, 0)
    arrive((2, 0), (6, 0))

    remote(
        pcode.at[pl.ds(1, PLANE - 1)], pcode.at[pl.ds(1, PLANE - 1)], pc_send, pc_recv, in_plane(1)
    ).wait_recv()
    p_to_smem = pltpu.make_async_copy(pcode, rsm, sm_sem.at[1])
    p_to_smem.start()
    p_to_smem.wait()
    for v in range(KV):
        key_copy(v).wait()

    units(0, 0, None)
    units(1, 0, None)
    arrive((3, 0), (5, 0))
    start_ring(1)
    units(0, 1, 7)
    arrive((4, 0))
    units(0, 2, 6)
    arrive((1, 1), (7, 1))
    units(0, 4, None, True)
    units(0, 5, None, True)
    units(0, 3, None, True)
    arrive((2, 1), (6, 1))

    def pick(s, h, t):
        owner = zsm[s, 0, OWNERS + h * TOPK + t]
        dx = lax.rem(lax.rem(owner, NX) - x + NX, NX)
        dy = lax.rem(lax.div(owner, NX * NZ) - y + NY, NY)
        dz = lax.rem(lax.rem(lax.div(owner, NX), NZ) - z + NZ, NZ)
        away = lax.div(dz + NZ - 1, NZ)
        return away, (dx + NX * dy) * (1 - away)

    def gather_levels(s, c):
        others = pl.ds(1, PLANE - 1)
        remote(
            rl[s][c].at[others], rl[s][c].at[others], ls_send.at[s], ls_recv.at[s, c], in_plane(1)
        ).wait_recv()

        def body(h, _):
            for t in range(TOPK):
                away, k = pick(s, h, t)
                lt[s, c, t, pl.ds(h, 1), :] = rl[s][c][k + PLANE * away]
            return 0

        lax.fori_loop(0, HEADS, body, 0)

    def weigh(c, heads, levels):
        top = functools.reduce(jnp.maximum, levels)
        parts = [jnp.exp(level - top) for level in levels]
        total = functools.reduce(jnp.add, parts)
        inverse = 1.0 / total
        for i, part in enumerate(parts):
            wt[c, i, heads] = part * inverse
        return top + jnp.log(total)

    def picked_levels(s, c, heads):
        return [lt[s, c, t, heads, :] for t in range(TOPK)]

    def picked_sum(s, c, h):
        total = None
        for t in range(TOPK):
            _, k = pick(s, h, t)
            term = wt[c, t, pl.ds(h, 1), :] * ret[s][c][k].astype(jnp.float32)
            total = term if total is None else total + term
        return total

    def wait_back(s, c):
        remote(
            ret[s][c].at[pl.ds(1, PLANE - 1)], ret[s][c].at[pl.ds(1, PLANE - 1)],
            rs_send.at[s], rs_recv.at[s, c], in_plane(1),
        ).wait_recv()

    def sum_copies(s, c, step):
        to = s + step
        heads = pl.ds(0, HEADS)
        if s == NZ // 2:
            heads = pl.ds(0 if step > 0 else HEADS // 2, HEADS // 2)
        way = 0 if step > 0 else 1
        return [
            remote(
                zacc.at[s, c, heads], zacc.at[to, c, heads], za_send.at[way, s, c],
                za_recv.at[to, c], along_z(step),
            ),
            remote(
                zl.at[s, c, heads], zl.at[to, c, heads], zl_send.at[way, s, c],
                zl_recv.at[to, c], along_z(step),
            ),
        ]

    def steps_from(s):
        return (1, -1) if s == NZ // 2 else (-1,) if s < NZ // 2 else (1,)

    def wait_sum(s, c, step):
        for copy in sum_copies(s - step, c, step):
            copy.wait_recv()

    def combine(c, s):
        gather_levels(s, c)
        wait_back(s, c)
        half = HEADS // 2
        if s == NZ // 2:
            parts = [(0, HEADS, False)]
        elif s == NZ // 2 + 1:
            parts = [(half, half, False), (0, half, True)]
        elif s == NZ // 2 - 1:
            parts = [(0, half, False), (half, half, True)]
        else:
            parts = [(0, HEADS, True)]
        for start, count, upstream in parts:
            heads = slice(start, start + count)
            levels = picked_levels(s, c, heads)
            if upstream:
                wait_sum(s, c, 1 if s > NZ // 2 else -1)
                levels.append(zl[s, c, heads])
            zl[s, c, heads] = weigh(c, heads, levels)

            def body(h, _, upstream=upstream):
                total = picked_sum(s, c, h)
                if upstream:
                    total += wt[c, TOPK, pl.ds(h, 1), :] * zacc[s, c, h].astype(jnp.float32)
                zacc[s, c, h] = total.astype(jnp.bfloat16)
                return 0

            lax.fori_loop(start, start + count, body, 0)
        for step in steps_from(s):
            for copy in sum_copies(s, c, step):
                copy.start()

    combine(0, 4)
    units(1, 1, 7)
    arrive((3, 1), (5, 1))
    combine(0, 5)
    combine(0, 3)
    send_back(0, 6, 2)
    arrive((4, 1))
    units(1, 2, 6)
    units(1, 5, 3)
    units(1, 4, None, True)
    send_back(1, 5, 3)
    combine(0, 6)
    combine(0, 2)
    send_back(0, 7, 1)
    combine(1, 4)
    combine(1, 5)
    combine(1, 3)
    send_back(1, 6, 2)
    combine(0, 7)
    combine(0, 1)
    send_back(1, 7, 1)
    combine(1, 6)
    combine(1, 2)
    send_back(0, 0)
    send_back(1, 0)
    combine(1, 7)
    combine(1, 1)
    for c in range(2):
        gather_levels(0, c)
        wait_back(0, c)
        wait_sum(0, c, -1)
        wait_sum(NZ, c, 1)
        every = slice(0, HEADS)
        weigh(c, every, picked_levels(0, c, every) + [zl[0, c], zl[NZ, c], own_l[c]])

        def finish(h, _, c=c):
            total = picked_sum(0, c, h)
            total += wt[c, TOPK, pl.ds(h, 1), :] * zacc[0, c, h].astype(jnp.float32)
            total += wt[c, TOPK + 1, pl.ds(h, 1), :] * zacc[NZ, c, h].astype(jnp.float32)
            total += wt[c, TOPK + 2, pl.ds(h, 1), :] * own_o[c, h]
            lanes = pl.ds(pl.multiple_of(h * HEAD_SIZE, HEAD_SIZE), HEAD_SIZE)
            out_ref[c * HALF : (c + 1) * HALF, lanes] = total.T.astype(jnp.bfloat16)
            return 0

        lax.fori_loop(0, HEADS, finish, 0)

    z_codes.wait_send()
    remote(
        pcode.at[pl.ds(1, PLANE - 1)], pcode.at[pl.ds(1, PLANE - 1)], pc_send, pc_recv, in_plane(1)
    ).wait_send()
    for copy in pair:
        copy.wait_send()
    for c in range(2):
        for s in range(NZ):
            for step in (1, -1):
                if s == 0 or (s != NZ // 2 and (s < NZ // 2) == (step > 0)):
                    for part in parts_to(s, step):
                        z_query(s, c, step, part).wait_send()
            if s > 0:
                for step in steps_from(s):
                    for copy in sum_copies(s, c, step):
                        copy.wait_send()
    others = pl.ds(1, PLANE - 1)
    for s in range(NZ):
        remote(
            tx.at[s, :, others], rx.at[s, :, others], tx_send.at[s], rx_recv.at[s, 0, 0], in_plane(1)
        ).wait_send()
        remote(
            rx.at[s, :, others], tx.at[s, :, others], rs_send.at[s], rs_recv.at[s, 0], in_plane(1)
        ).wait_send()
        remote(
            lout.at[s, :, others], lout.at[s, :, others], ls_send.at[s], ls_recv.at[s, 0], in_plane(1)
        ).wait_send()


def exchange(q, ck, cv, kp, vp, code):
    dma = pltpu.SemaphoreType.DMA
    bf16, f32 = jnp.bfloat16, jnp.float32
    half = (HEADS, HEAD_SIZE, HALF)
    scratch = [pltpu.VMEM(half, bf16)] * (2 * NZ)
    scratch += [pltpu.VMEM((PLANE, HEAD_SIZE, HALF), bf16)] * (2 * NZ)
    scratch += [pltpu.VMEM((PLANE + 1, 1, HALF), f32)] * (2 * NZ)
    scratch += [
        pltpu.VMEM((KV * OWNED, KEY_BLOCK_SIZE, HEAD_SIZE), bf16),
        pltpu.VMEM((2, OWNED, KEY_BLOCK_SIZE, HEAD_SIZE), bf16),
        pltpu.VMEM((KV * OWNED, HEAD_SIZE, KEY_BLOCK_SIZE), bf16),
        pltpu.VMEM((NZ, 2, PLANE, HEAD_SIZE, HALF), bf16),
        pltpu.VMEM((NZ, 2, PLANE, HEAD_SIZE, HALF), bf16),
        pltpu.VMEM((NZ, 2, PLANE, 1, HALF), f32),
        pltpu.VMEM((NZ + 1, 2) + half, bf16),
        pltpu.VMEM((NZ + 1, 2, HEADS, HALF), f32),
        pltpu.VMEM((2,) + half, f32),
        pltpu.VMEM((2, HEADS, HALF), f32),
        pltpu.VMEM((ROWS, KV * HEAD_SIZE), bf16),
        pltpu.VMEM((KV, HEAD_SIZE, ROWS), bf16),
        pltpu.VMEM((KV, HEAD_SIZE, ROWS), bf16),
        pltpu.VMEM((NZ, 2, TOPK, HEADS, HALF), f32),
        pltpu.VMEM((2, TOPK + 3, HEADS, HALF), f32),
        pltpu.VMEM((NZ, 1, 2 * OWNERS), jnp.int32),
        pltpu.VMEM((PLANE, NZ, 1, OWNERS), jnp.int32),
        pltpu.SMEM((NZ, 1, 2 * OWNERS), jnp.int32),
        pltpu.SMEM((PLANE, NZ, 1, OWNERS), jnp.int32),
        dma((KV,)), dma((KV,)),
        dma((2, NZ, 2, 2)), dma((NZ, 2, 2)),
        dma, dma, dma, dma, dma((2,)),
        dma((2,)), dma((2,)),
        dma((NZ,)), dma((NZ, 2, PLANE)),
        dma((NZ,)), dma((NZ, 2)),
        dma((NZ,)), dma((NZ, 2)),
        dma((2, NZ, 2)), dma((NZ + 1, 2)), dma((2, NZ, 2)), dma((NZ + 1, 2)),
    ]
    vmem = pl.BlockSpec(memory_space=pltpu.VMEM)
    hbm = pl.BlockSpec(memory_space=pl.ANY)
    return pl.pallas_call(
        kernel,
        out_shape=jax.ShapeDtypeStruct((ROWS, HEADS * HEAD_SIZE), bf16),
        in_specs=[vmem, vmem, vmem, hbm, hbm, vmem, pl.BlockSpec(memory_space=pltpu.SMEM)],
        out_specs=vmem,
        scratch_shapes=scratch,
        compiler_params=pltpu.CompilerParams(
            collective_id=0, has_side_effects=True, vmem_limit_bytes=62 << 20
        ),
        name="attend",
    )(q, ck, cv, kp, vp, code, code)


def local(queries, current_keys, current_values, cached_key_pages, cached_value_pages, picks):
    chosen = picks.reshape(HEADS * TOPK)
    owner = chosen // OWNED
    head = jnp.arange(HEADS * TOPK) // TOPK
    table = head // GROUP * OWNED + chosen % OWNED
    value = head + HEADS * table
    by_owner = jnp.sum(
        jnp.where(owner[None, :] == jnp.arange(OWNERS)[:, None], value[None, :], 0), axis=1
    )
    code = jnp.concatenate([by_owner, jnp.pad(owner, (0, OWNERS - HEADS * TOPK))])
    return exchange(
        queries,
        current_keys,
        current_values,
        cached_key_pages.reshape(OWNED, KEY_BLOCK_SIZE, KV * HEAD_SIZE),
        cached_value_pages.reshape(OWNED, KEY_BLOCK_SIZE, KV * HEAD_SIZE),
        code.reshape(1, 2 * OWNERS).astype(jnp.int32),
    )


def solution(mesh):
    placed = (
        P("ctx", "kvh"),
        P("ctx", "kvh"),
        P("ctx", "kvh"),
        P("ctx", "kvh"),
        P("ctx", "kvh"),
        P("ctx", "kvh", None),
    )
    return jax.shard_map(
        local, mesh=mesh, in_specs=placed, out_specs=P("ctx", "kvh"), check_vma=False
    )
```

```python
import functools

import jax
import jax.numpy as jnp
from jax import lax
from jax.experimental import pallas as pl
from jax.experimental.pallas import tpu as pltpu
from jax.sharding import PartitionSpec as P

HEAD_SIZE = 128
KEY_BLOCK_SIZE = 512
TOPK = 3
MESH = pl.DeviceIdType.MESH
NX, NY, NZ = 4, 4, 8
PLANE = NX * NY
HEADS = 16
KV = 4
GROUP = HEADS // KV
OWNED = 8
ROWS = 256
HALF = 128
OWNERS = 128
SCALE = HEAD_SIZE**-0.5
SCALE2 = SCALE * 1.4426950408889634
LOW = -1e30


def kernel(*refs):
    (q_ref, ck_ref, cv_ref, kp_ref, vp_ref, code_ref, csm, out_ref), refs = refs[:8], refs[8:]
    zq, refs = [refs[2 * s : 2 * s + 2] for s in range(NZ)], refs[2 * NZ :]
    ret, refs = [refs[2 * s : 2 * s + 2] for s in range(NZ)], refs[2 * NZ :]
    rl, refs = [refs[2 * s : 2 * s + 2] for s in range(NZ)], refs[2 * NZ :]
    (
        kbuf, vstage, vbuf, tx, rx, lout, zacc, zl, own_o, own_l, pk, pvt, cvt, lt, wt,
        zcode, pcode, zsm, rsm,
        k_sem, v_sem, zq_send, zq_recv, zc_send, zc_recv, pc_send, pc_recv, sm_sem,
        xp_send, xp_recv, tx_send, rx_recv, rs_send, rs_recv, ls_send, ls_recv,
        za_send, za_recv, zl_send, zl_recv,
    ) = refs
    me = lax.axis_index("ctx")
    core = lax.axis_index("kvh")
    x = lax.rem(me, NX)
    z = lax.rem(me // NX, NZ)
    y = me // (NX * NZ)

    def in_plane(k):
        return (
            lax.rem(y + k // NX, NY) * (NX * NZ) + z * NX + lax.rem(x + lax.rem(k, NX), NX),
            core,
        )

    def opposite(k):
        return (
            lax.rem(y + NY - k // NX, NY) * (NX * NZ)
            + z * NX
            + lax.rem(x + NX - lax.rem(k, NX), NX),
            core,
        )

    def along_z(d):
        return (y * (NX * NZ) + lax.rem(z + d + NZ, NZ) * NX + x, core)

    def owner_at(k):
        return in_plane(k)[0]

    def remote(src, dst, send, recv, device):
        return pltpu.make_async_remote_copy(
            src_ref=src,
            dst_ref=dst,
            send_sem=send,
            recv_sem=recv,
            device_id=device,
            device_id_type=MESH,
        )

    def key_copy(v):
        return pltpu.make_async_copy(
            kp_ref.at[:, :, pl.ds(v * HEAD_SIZE, HEAD_SIZE)],
            kbuf.at[pl.ds(v * OWNED, OWNED)],
            k_sem.at[v],
        )

    def value_copy(v):
        return pltpu.make_async_copy(
            vp_ref.at[:, :, pl.ds(v * HEAD_SIZE, HEAD_SIZE)], vstage.at[v % 2], v_sem.at[v]
        )

    value_copy(0).start()
    value_copy(1).start()
    for v in range(KV):
        key_copy(v).start()

    barrier = pltpu.get_barrier_semaphore()
    for k in range(1, PLANE):
        pl.semaphore_signal(barrier, inc=1, device_id=in_plane(k), device_id_type=MESH)
    for d in range(1, NZ):
        pl.semaphore_signal(barrier, inc=1, device_id=along_z(d), device_id_type=MESH)

    for c in range(2):
        for h in range(HEADS):
            zq[0][c][h] = q_ref[
                c * HALF : (c + 1) * HALF, h * HEAD_SIZE : (h + 1) * HEAD_SIZE
            ].T
    for v in range(KV):
        cvt[v] = cv_ref[:, v * HEAD_SIZE : (v + 1) * HEAD_SIZE].T
    zcode[0] = code_ref[...]
    pl.semaphore_wait(barrier, PLANE - 1 + NZ - 1)

    def z_query(s, c, step, part):
        to = (s + step) % NZ
        heads = pl.ds(part * (HEADS // 2), HEADS // 2)
        return remote(
            zq[s][c].at[heads],
            zq[to][c].at[heads],
            zq_send.at[0 if step > 0 else 1, s, c, part],
            zq_recv.at[to, c, part],
            along_z(step),
        )

    def parts_to(s, step):
        return (0, 1) if (s + step) % NZ != NZ // 2 else (0,) if step > 0 else (1,)

    def start_ring(c):
        for part in range(2):
            for step in (1, -1):
                z_query(0, c, step, part).start()

    start_ring(0)

    def z_code(d):
        return remote(zcode.at[0], zcode.at[d], zc_send, zc_recv, along_z(d))

    for d in range(1, NZ):
        z_code(d).start()

    z_codes = remote(
        zcode.at[pl.ds(1, NZ - 1)], zcode.at[pl.ds(1, NZ - 1)], zc_send, zc_recv, along_z(1)
    )
    def query_copy(s, c, k):
        return remote(
            tx.at[s, c, k], rx.at[s, c, k], tx_send.at[s], rx_recv.at[s, c, k], in_plane(k)
        )

    def send_out(s, c):
        def head_for(k):
            owner = owner_at(k)
            return lax.rem(csm[0, owner] if s == 0 else zsm[s, 0, owner], HEADS)

        rx[s, c, 0] = zq[s][c][head_for(0)]

        def body(k, _):
            tx[s, c, k] = zq[s][c][head_for(k)]
            query_copy(s, c, k).start()
            return 0

        lax.fori_loop(1, PLANE, body, 0)

    def pass_on(s, c):
        for step in (1, -1):
            if s == NZ // 2 or (s < NZ // 2) == (step > 0):
                for part in parts_to(s - step, step):
                    z_query((s - step) % NZ, c, step, part).wait_recv()
                    if s != NZ // 2 and part in parts_to(s, step):
                        z_query(s, c, step, part).start()

    def arrive(*pairs):
        for s, c in pairs:
            pass_on(s, c)
        for s, c in pairs:
            send_out(s, c)

    def attend(keys, queries, values):
        scores = jnp.dot(keys, queries, preferred_element_type=jnp.float32)
        top = jnp.max(scores, axis=0, keepdims=True)
        weights = jnp.exp2(scores * SCALE2 - top * SCALE2)
        total = jnp.sum(weights, axis=0, keepdims=True)
        out = jnp.dot(values, weights.astype(jnp.bfloat16), preferred_element_type=jnp.float32)
        return out * (1.0 / total), top * SCALE + jnp.log(total)

    def unit(s, c, k):
        table = lax.div(rsm[k, s, 0, me], HEADS)
        out, level = attend(kbuf[table], rx[s, c, k], vbuf[table])
        rx[s, c, k] = out.astype(jnp.bfloat16)
        lout[s, c, k] = level

    def back_copy(s, c, k):
        return remote(
            rx.at[s, c, k], ret[s][c].at[k], rs_send.at[s], rs_recv.at[s, c], opposite(k)
        )

    def level_copy(s, c, k):
        return remote(
            lout.at[s, c, k], rl[s][c].at[k], ls_send.at[s], ls_recv.at[s, c], opposite(k)
        )

    def units(c, a, b, then=False):
        count = 1 if b is None else 2

        def body(j, _):
            s = a if b is None else a + (b - a) * lax.div(j, PLANE // 4)
            for i in range(4):
                k = lax.rem(j, PLANE // 4) * 4 + i

                def wait(k=k):
                    query_copy(s, c, k).wait_recv()

                if i == 0:
                    pl.when(k > 0)(wait)
                else:
                    wait()
            for i in range(4):
                unit(s, c, lax.rem(j, PLANE // 4) * 4 + i)
            for i in range(4 if then else 0):
                k = lax.rem(j, PLANE // 4) * 4 + i

                def start(k=k):
                    level_copy(s, c, k).start()
                    back_copy(s, c, k).start()

                if i == 0:
                    pl.when(k > 0)(start)
                else:
                    start()
            return 0

        lax.fori_loop(0, count * PLANE // 4, body, 0)
        for s in (a, b)[:count]:
            ret[s][c][0] = rx[s, c, 0]
            rl[s][c][0] = lout[s, c, 0]
            rl[s][c][PLANE] = jnp.full((1, HALF), LOW, jnp.float32)

    def send_back(c, *slots):
        for s in slots:

            def body(k, _, s=s):
                level_copy(s, c, k).start()
                back_copy(s, c, k).start()
                return 0

            lax.fori_loop(1, PLANE, body, 0)

    send_out(0, 0)
    send_out(0, 1)
    odd = lax.rem(me, 2)
    partner = (me + 1 - 2 * odd, core)
    pair = [
        remote(ck_ref, pk, xp_send.at[0], xp_recv.at[0], partner),
        remote(cvt, pvt, xp_send.at[1], xp_recv.at[1], partner),
    ]

    @pl.when(odd == 0)
    def _():
        for copy in pair:
            copy.start()
        pvt[...] = jnp.zeros_like(pvt)


    for v in range(KV):
        value_copy(v).wait()

        def turn(w, _, v=v):
            vbuf[v * OWNED + w] = vstage[v % 2, w].T
            return 0

        lax.fori_loop(0, OWNED, turn, 0)
        if v + 2 < KV:
            value_copy(v + 2).start()

    z_codes.wait_recv()

    def p_code(k):
        return remote(
            zcode.at[:, :, pl.ds(0, OWNERS)], pcode.at[k], pc_send, pc_recv, in_plane(k)
        )

    def start_p_code(k, _):
        p_code(k).start()
        return 0

    lax.fori_loop(1, PLANE, start_p_code, 0)
    pcode[0] = zcode[:, :, :OWNERS]
    z_to_smem = pltpu.make_async_copy(zcode, zsm, sm_sem.at[0])
    z_to_smem.start()
    z_to_smem.wait()

    arrive((1, 0), (7, 0))

    @pl.when(odd == 1)
    def _():
        for copy in pair:
            copy.wait_recv()


    def own(h, _):
        v = h // GROUP
        lanes = pl.ds(pl.multiple_of(v * HEAD_SIZE, HEAD_SIZE), HEAD_SIZE)
        queries = jnp.concatenate([zq[0][0][h], zq[0][1][h]], axis=1)
        before = jnp.dot(pk[:, lanes], queries, preferred_element_type=jnp.float32)
        here = jnp.dot(ck_ref[:, lanes], queries, preferred_element_type=jnp.float32)
        key_pos = lax.broadcasted_iota(jnp.int32, (ROWS, ROWS), 0)
        query_pos = lax.broadcasted_iota(jnp.int32, (ROWS, ROWS), 1)
        before = jnp.where(odd == 1, before, LOW)
        here = jnp.where(key_pos <= query_pos, here, LOW)
        top = jnp.maximum(
            jnp.max(before, axis=0, keepdims=True), jnp.max(here, axis=0, keepdims=True)
        )
        weights_before = jnp.exp2((before - top) * SCALE2)
        weights_here = jnp.exp2((here - top) * SCALE2)
        total = jnp.sum(weights_before, axis=0, keepdims=True) + jnp.sum(
            weights_here, axis=0, keepdims=True
        )
        out = jnp.dot(pvt[v], weights_before.astype(jnp.bfloat16), preferred_element_type=jnp.float32)
        out += jnp.dot(cvt[v], weights_here.astype(jnp.bfloat16), preferred_element_type=jnp.float32)
        out = out * (1.0 / total)
        level = top * SCALE + jnp.log(total)
        for c in range(2):
            own_o[c, h] = out[:, c * HALF : (c + 1) * HALF]
            own_l[c, pl.ds(h, 1), :] = level[:, c * HALF : (c + 1) * HALF]
        return 0

    lax.fori_loop(0, HEADS, own, 0, unroll=2)
    arrive((2, 0), (6, 0))

    remote(
        pcode.at[pl.ds(1, PLANE - 1)], pcode.at[pl.ds(1, PLANE - 1)], pc_send, pc_recv, in_plane(1)
    ).wait_recv()
    p_to_smem = pltpu.make_async_copy(pcode, rsm, sm_sem.at[1])
    p_to_smem.start()
    p_to_smem.wait()
    for v in range(KV):
        key_copy(v).wait()

    units(0, 0, None)
    units(1, 0, None)
    arrive((3, 0), (5, 0))
    start_ring(1)
    units(0, 1, 7)
    arrive((4, 0))
    units(0, 2, 6)
    arrive((1, 1), (7, 1))
    units(0, 4, None, True)
    units(0, 5, None, True)
    units(0, 3, None, True)
    arrive((2, 1), (6, 1))

    def pick(s, h, t):
        owner = zsm[s, 0, OWNERS + h * TOPK + t]
        dx = lax.rem(lax.rem(owner, NX) - x + NX, NX)
        dy = lax.rem(lax.div(owner, NX * NZ) - y + NY, NY)
        dz = lax.rem(lax.rem(lax.div(owner, NX), NZ) - z + NZ, NZ)
        away = lax.div(dz + NZ - 1, NZ)
        return away, (dx + NX * dy) * (1 - away)

    def gather_levels(s, c):
        others = pl.ds(1, PLANE - 1)
        remote(
            rl[s][c].at[others], rl[s][c].at[others], ls_send.at[s], ls_recv.at[s, c], in_plane(1)
        ).wait_recv()

        def body(h, _):
            for t in range(TOPK):
                away, k = pick(s, h, t)
                lt[s, c, t, pl.ds(h, 1), :] = rl[s][c][k + PLANE * away]
            return 0

        lax.fori_loop(0, HEADS, body, 0, unroll=4)

    def weigh(c, heads, levels):
        top = functools.reduce(jnp.maximum, levels)
        parts = [jnp.exp(level - top) for level in levels]
        total = functools.reduce(jnp.add, parts)
        inverse = 1.0 / total
        for i, part in enumerate(parts):
            wt[c, i, heads] = part * inverse
        return top + jnp.log(total)

    def picked_levels(s, c, heads):
        return [lt[s, c, t, heads, :] for t in range(TOPK)]

    def picked_sum(s, c, h):
        total = None
        for t in range(TOPK):
            _, k = pick(s, h, t)
            term = wt[c, t, pl.ds(h, 1), :] * ret[s][c][k].astype(jnp.float32)
            total = term if total is None else total + term
        return total

    def wait_back(s, c):
        remote(
            ret[s][c].at[pl.ds(1, PLANE - 1)], ret[s][c].at[pl.ds(1, PLANE - 1)],
            rs_send.at[s], rs_recv.at[s, c], in_plane(1),
        ).wait_recv()

    def sum_copies(s, c, step):
        to = s + step
        heads = pl.ds(0, HEADS)
        if s == NZ // 2:
            heads = pl.ds(0 if step > 0 else HEADS // 2, HEADS // 2)
        way = 0 if step > 0 else 1
        return [
            remote(
                zacc.at[s, c, heads], zacc.at[to, c, heads], za_send.at[way, s, c],
                za_recv.at[to, c], along_z(step),
            ),
            remote(
                zl.at[s, c, heads], zl.at[to, c, heads], zl_send.at[way, s, c],
                zl_recv.at[to, c], along_z(step),
            ),
        ]

    def steps_from(s):
        return (1, -1) if s == NZ // 2 else (-1,) if s < NZ // 2 else (1,)

    def wait_sum(s, c, step):
        for copy in sum_copies(s - step, c, step):
            copy.wait_recv()

    def combine(c, s):
        gather_levels(s, c)
        wait_back(s, c)
        half = HEADS // 2
        if s == NZ // 2:
            parts = [(0, HEADS, False)]
        elif s == NZ // 2 + 1:
            parts = [(half, half, False), (0, half, True)]
        elif s == NZ // 2 - 1:
            parts = [(0, half, False), (half, half, True)]
        else:
            parts = [(0, HEADS, True)]
        for start, count, upstream in parts:
            heads = slice(start, start + count)
            levels = picked_levels(s, c, heads)
            if upstream:
                wait_sum(s, c, 1 if s > NZ // 2 else -1)
                levels.append(zl[s, c, heads])
            zl[s, c, heads] = weigh(c, heads, levels)

            def body(h, _, upstream=upstream):
                total = picked_sum(s, c, h)
                if upstream:
                    total += wt[c, TOPK, pl.ds(h, 1), :] * zacc[s, c, h].astype(jnp.float32)
                zacc[s, c, h] = total.astype(jnp.bfloat16)
                return 0

            lax.fori_loop(start, start + count, body, 0, unroll=4)
        for step in steps_from(s):
            for copy in sum_copies(s, c, step):
                copy.start()

    combine(0, 4)
    arrive((3, 1), (5, 1))
    arrive((4, 1))
    units(1, 1, 7)
    combine(0, 5)
    combine(0, 3)
    send_back(0, 6, 2)
    units(1, 2, 6)
    units(1, 5, 3)
    units(1, 4, None, True)
    send_back(1, 5, 3)
    combine(0, 6)
    combine(0, 2)
    send_back(0, 7, 1)
    combine(1, 4)
    combine(1, 5)
    combine(1, 3)
    send_back(1, 6, 2)
    combine(0, 7)
    combine(0, 1)
    send_back(1, 7, 1)
    combine(1, 6)
    combine(1, 2)
    send_back(0, 0)
    send_back(1, 0)
    combine(1, 7)
    combine(1, 1)
    for c in range(2):
        gather_levels(0, c)
        wait_back(0, c)
        wait_sum(0, c, -1)
        wait_sum(NZ, c, 1)
        every = slice(0, HEADS)
        weigh(c, every, picked_levels(0, c, every) + [zl[0, c], zl[NZ, c], own_l[c]])

        def finish(h, _, c=c):
            total = picked_sum(0, c, h)
            total += wt[c, TOPK, pl.ds(h, 1), :] * zacc[0, c, h].astype(jnp.float32)
            total += wt[c, TOPK + 1, pl.ds(h, 1), :] * zacc[NZ, c, h].astype(jnp.float32)
            total += wt[c, TOPK + 2, pl.ds(h, 1), :] * own_o[c, h]
            lanes = pl.ds(pl.multiple_of(h * HEAD_SIZE, HEAD_SIZE), HEAD_SIZE)
            out_ref[c * HALF : (c + 1) * HALF, lanes] = total.T.astype(jnp.bfloat16)
            return 0

        lax.fori_loop(0, HEADS, finish, 0, unroll=4)

    z_codes.wait_send()
    remote(
        pcode.at[pl.ds(1, PLANE - 1)], pcode.at[pl.ds(1, PLANE - 1)], pc_send, pc_recv, in_plane(1)
    ).wait_send()

    @pl.when(odd == 0)
    def _():
        for copy in pair:
            copy.wait_send()

    for c in range(2):
        for s in range(NZ):
            for step in (1, -1):
                if s == 0 or (s != NZ // 2 and (s < NZ // 2) == (step > 0)):
                    for part in parts_to(s, step):
                        z_query(s, c, step, part).wait_send()
            if s > 0:
                for step in steps_from(s):
                    for copy in sum_copies(s, c, step):
                        copy.wait_send()
    others = pl.ds(1, PLANE - 1)
    for s in range(NZ):
        remote(
            tx.at[s, :, others], rx.at[s, :, others], tx_send.at[s], rx_recv.at[s, 0, 0], in_plane(1)
        ).wait_send()
        remote(
            rx.at[s, :, others], tx.at[s, :, others], rs_send.at[s], rs_recv.at[s, 0], in_plane(1)
        ).wait_send()
        remote(
            lout.at[s, :, others], lout.at[s, :, others], ls_send.at[s], ls_recv.at[s, 0], in_plane(1)
        ).wait_send()


def exchange(q, ck, cv, kp, vp, code):
    dma = pltpu.SemaphoreType.DMA
    bf16, f32 = jnp.bfloat16, jnp.float32
    half = (HEADS, HEAD_SIZE, HALF)
    scratch = [pltpu.VMEM(half, bf16)] * (2 * NZ)
    scratch += [pltpu.VMEM((PLANE, HEAD_SIZE, HALF), bf16)] * (2 * NZ)
    scratch += [pltpu.VMEM((PLANE + 1, 1, HALF), f32)] * (2 * NZ)
    scratch += [
        pltpu.VMEM((KV * OWNED, KEY_BLOCK_SIZE, HEAD_SIZE), bf16),
        pltpu.VMEM((2, OWNED, KEY_BLOCK_SIZE, HEAD_SIZE), bf16),
        pltpu.VMEM((KV * OWNED, HEAD_SIZE, KEY_BLOCK_SIZE), bf16),
        pltpu.VMEM((NZ, 2, PLANE, HEAD_SIZE, HALF), bf16),
        pltpu.VMEM((NZ, 2, PLANE, HEAD_SIZE, HALF), bf16),
        pltpu.VMEM((NZ, 2, PLANE, 1, HALF), f32),
        pltpu.VMEM((NZ + 1, 2) + half, bf16),
        pltpu.VMEM((NZ + 1, 2, HEADS, HALF), f32),
        pltpu.VMEM((2,) + half, f32),
        pltpu.VMEM((2, HEADS, HALF), f32),
        pltpu.VMEM((ROWS, KV * HEAD_SIZE), bf16),
        pltpu.VMEM((KV, HEAD_SIZE, ROWS), bf16),
        pltpu.VMEM((KV, HEAD_SIZE, ROWS), bf16),
        pltpu.VMEM((NZ, 2, TOPK, HEADS, HALF), f32),
        pltpu.VMEM((2, TOPK + 3, HEADS, HALF), f32),
        pltpu.VMEM((NZ, 1, 2 * OWNERS), jnp.int32),
        pltpu.VMEM((PLANE, NZ, 1, OWNERS), jnp.int32),
        pltpu.SMEM((NZ, 1, 2 * OWNERS), jnp.int32),
        pltpu.SMEM((PLANE, NZ, 1, OWNERS), jnp.int32),
        dma((KV,)), dma((KV,)),
        dma((2, NZ, 2, 2)), dma((NZ, 2, 2)),
        dma, dma, dma, dma, dma((2,)),
        dma((2,)), dma((2,)),
        dma((NZ,)), dma((NZ, 2, PLANE)),
        dma((NZ,)), dma((NZ, 2)),
        dma((NZ,)), dma((NZ, 2)),
        dma((2, NZ, 2)), dma((NZ + 1, 2)), dma((2, NZ, 2)), dma((NZ + 1, 2)),
    ]
    vmem = pl.BlockSpec(memory_space=pltpu.VMEM)
    hbm = pl.BlockSpec(memory_space=pl.ANY)
    return pl.pallas_call(
        kernel,
        out_shape=jax.ShapeDtypeStruct((ROWS, HEADS * HEAD_SIZE), bf16),
        in_specs=[vmem, vmem, vmem, hbm, hbm, vmem, pl.BlockSpec(memory_space=pltpu.SMEM)],
        out_specs=vmem,
        scratch_shapes=scratch,
        compiler_params=pltpu.CompilerParams(
            collective_id=0, has_side_effects=True, vmem_limit_bytes=62 << 20
        ),
        name="attend",
    )(q, ck, cv, kp, vp, code, code)


def local(queries, current_keys, current_values, cached_key_pages, cached_value_pages, picks):
    chosen = picks.reshape(HEADS * TOPK)
    owner = chosen // OWNED
    head = jnp.arange(HEADS * TOPK) // TOPK
    table = head // GROUP * OWNED + chosen % OWNED
    value = head + HEADS * table
    by_owner = jnp.sum(
        jnp.where(owner[None, :] == jnp.arange(OWNERS)[:, None], value[None, :], 0), axis=1
    )
    code = jnp.concatenate([by_owner, jnp.pad(owner, (0, OWNERS - HEADS * TOPK))])
    return exchange(
        queries,
        current_keys,
        current_values,
        cached_key_pages.reshape(OWNED, KEY_BLOCK_SIZE, KV * HEAD_SIZE),
        cached_value_pages.reshape(OWNED, KEY_BLOCK_SIZE, KV * HEAD_SIZE),
        code.reshape(1, 2 * OWNERS).astype(jnp.int32),
    )


def solution(mesh):
    placed = (
        P("ctx", "kvh"),
        P("ctx", "kvh"),
        P("ctx", "kvh"),
        P("ctx", "kvh"),
        P("ctx", "kvh"),
        P("ctx", "kvh", None),
    )
    return jax.shard_map(
        local, mesh=mesh, in_specs=placed, out_specs=P("ctx", "kvh"), check_vma=False
    )
```

```python
import functools

import jax
import jax.numpy as jnp
from jax import lax
from jax.experimental import pallas as pl
from jax.experimental.pallas import tpu as pltpu
from jax.sharding import PartitionSpec as P

HEAD_SIZE = 128
KEY_BLOCK_SIZE = 512
TOPK = 3
MESH = pl.DeviceIdType.MESH
NX, NY, NZ = 4, 4, 8
PLANE = NX * NY
HEADS = 16
KV = 4
GROUP = HEADS // KV
OWNED = 8
ROWS = 256
HALF = 128
OWNERS = 128
SCALE = HEAD_SIZE**-0.5
SCALE2 = SCALE * 1.4426950408889634
LOW = -1e30


def kernel(*refs):
    (q_ref, ck_ref, cv_ref, kp_ref, vp_ref, code_ref, csm, out_ref), refs = refs[:8], refs[8:]
    zq, refs = [refs[2 * s : 2 * s + 2] for s in range(NZ)], refs[2 * NZ :]
    ret, refs = [refs[2 * s : 2 * s + 2] for s in range(NZ)], refs[2 * NZ :]
    rl, refs = [refs[2 * s : 2 * s + 2] for s in range(NZ)], refs[2 * NZ :]
    (
        kbuf, vstage, vbuf, tx, rx, lout, zacc, zl, own_o, own_l, pk, pvt, cvt, lt, wt,
        zcode, pcode, zsm, rsm,
        k_sem, v_sem, zq_send, zq_recv, zc_send, zc_recv, pc_send, pc_recv, sm_sem,
        xp_send, xp_recv, tx_send, rx_recv, rs_send, rs_recv, ls_send, ls_recv,
        za_send, za_recv, zl_send, zl_recv,
    ) = refs
    me = lax.axis_index("ctx")
    core = lax.axis_index("kvh")
    x = lax.rem(me, NX)
    z = lax.rem(me // NX, NZ)
    y = me // (NX * NZ)

    def in_plane(k):
        return (
            lax.rem(y + k // NX, NY) * (NX * NZ) + z * NX + lax.rem(x + lax.rem(k, NX), NX),
            core,
        )

    def opposite(k):
        return (
            lax.rem(y + NY - k // NX, NY) * (NX * NZ)
            + z * NX
            + lax.rem(x + NX - lax.rem(k, NX), NX),
            core,
        )

    def along_z(d):
        return (y * (NX * NZ) + lax.rem(z + d + NZ, NZ) * NX + x, core)

    def owner_at(k):
        return in_plane(k)[0]

    def remote(src, dst, send, recv, device):
        return pltpu.make_async_remote_copy(
            src_ref=src,
            dst_ref=dst,
            send_sem=send,
            recv_sem=recv,
            device_id=device,
            device_id_type=MESH,
        )

    def key_copy(v):
        return pltpu.make_async_copy(
            kp_ref.at[:, :, pl.ds(v * HEAD_SIZE, HEAD_SIZE)],
            kbuf.at[pl.ds(v * OWNED, OWNED)],
            k_sem.at[v],
        )

    def value_copy(v):
        return pltpu.make_async_copy(
            vp_ref.at[:, :, pl.ds(v * HEAD_SIZE, HEAD_SIZE)], vstage.at[v % 2], v_sem.at[v]
        )

    value_copy(0).start()
    value_copy(1).start()
    for v in range(KV):
        key_copy(v).start()

    barrier = pltpu.get_barrier_semaphore()
    for k in range(1, PLANE):
        pl.semaphore_signal(barrier, inc=1, device_id=in_plane(k), device_id_type=MESH)
    for d in range(1, NZ):
        pl.semaphore_signal(barrier, inc=1, device_id=along_z(d), device_id_type=MESH)

    for c in range(2):
        for h in range(HEADS):
            zq[0][c][h] = q_ref[
                c * HALF : (c + 1) * HALF, h * HEAD_SIZE : (h + 1) * HEAD_SIZE
            ].T
    for v in range(KV):
        cvt[v] = cv_ref[:, v * HEAD_SIZE : (v + 1) * HEAD_SIZE].T
    zcode[0] = code_ref[...]
    pl.semaphore_wait(barrier, PLANE - 1 + NZ - 1)

    def z_query(s, c, step, part):
        to = (s + step) % NZ
        heads = pl.ds(part * (HEADS // 2), HEADS // 2)
        return remote(
            zq[s][c].at[heads],
            zq[to][c].at[heads],
            zq_send.at[0 if step > 0 else 1, s, c, part],
            zq_recv.at[to, c, part],
            along_z(step),
        )

    def parts_to(s, step):
        return (0, 1) if (s + step) % NZ != NZ // 2 else (0,) if step > 0 else (1,)

    def start_ring(c):
        for part in range(2):
            for step in (1, -1):
                z_query(0, c, step, part).start()

    start_ring(0)

    def z_code(d):
        return remote(zcode.at[0], zcode.at[d], zc_send, zc_recv, along_z(d))

    for d in range(1, NZ):
        z_code(d).start()

    z_codes = remote(
        zcode.at[pl.ds(1, NZ - 1)], zcode.at[pl.ds(1, NZ - 1)], zc_send, zc_recv, along_z(1)
    )
    def query_copy(s, c, k):
        return remote(
            tx.at[s, c, k], rx.at[s, c, k], tx_send.at[s], rx_recv.at[s, c, k], in_plane(k)
        )

    def send_out(s, c):
        def head_for(k):
            owner = owner_at(k)
            return lax.rem(csm[0, owner] if s == 0 else zsm[s, 0, owner], HEADS)

        rx[s, c, 0] = zq[s][c][head_for(0)]

        def body(k, _):
            tx[s, c, k] = zq[s][c][head_for(k)]
            query_copy(s, c, k).start()
            return 0

        lax.fori_loop(1, PLANE, body, 0)

    def pass_on(s, c):
        for step in (1, -1):
            if s == NZ // 2 or (s < NZ // 2) == (step > 0):
                for part in parts_to(s - step, step):
                    z_query((s - step) % NZ, c, step, part).wait_recv()
                    if s != NZ // 2 and part in parts_to(s, step):
                        z_query(s, c, step, part).start()

    def arrive(*pairs):
        for s, c in pairs:
            pass_on(s, c)
        for s, c in pairs:
            send_out(s, c)

    def attend(keys, queries, values):
        scores = jnp.dot(keys, queries, preferred_element_type=jnp.float32)
        top = jnp.max(scores, axis=0, keepdims=True)
        weights = jnp.exp2(scores * SCALE2 - top * SCALE2)
        total = jnp.sum(weights, axis=0, keepdims=True)
        out = jnp.dot(values, weights.astype(jnp.bfloat16), preferred_element_type=jnp.float32)
        return out * (1.0 / total), top * SCALE + jnp.log(total)

    def unit(s, c, k):
        table = lax.div(rsm[k, s, 0, me], HEADS)
        out, level = attend(kbuf[table], rx[s, c, k], vbuf[table])
        rx[s, c, k] = out.astype(jnp.bfloat16)
        lout[s, c, k] = level

    def back_copy(s, c, k):
        return remote(
            rx.at[s, c, k], ret[s][c].at[k], rs_send.at[s], rs_recv.at[s, c], opposite(k)
        )

    def level_copy(s, c, k):
        return remote(
            lout.at[s, c, k], rl[s][c].at[k], ls_send.at[s], ls_recv.at[s, c], opposite(k)
        )

    def units(c, a, b, then=False):
        count = 1 if b is None else 2

        def body(j, _):
            s = a if b is None else a + (b - a) * lax.div(j, PLANE // 4)
            for i in range(4):
                k = lax.rem(j, PLANE // 4) * 4 + i

                def wait(k=k):
                    query_copy(s, c, k).wait_recv()

                if i == 0:
                    pl.when(k > 0)(wait)
                else:
                    wait()
            for i in range(4):
                unit(s, c, lax.rem(j, PLANE // 4) * 4 + i)
            for i in range(4 if then else 0):
                k = lax.rem(j, PLANE // 4) * 4 + i

                def start(k=k):
                    level_copy(s, c, k).start()
                    back_copy(s, c, k).start()

                if i == 0:
                    pl.when(k > 0)(start)
                else:
                    start()
            return 0

        lax.fori_loop(0, count * PLANE // 4, body, 0)
        for s in (a, b)[:count]:
            ret[s][c][0] = rx[s, c, 0]
            rl[s][c][0] = lout[s, c, 0]
            rl[s][c][PLANE] = jnp.full((1, HALF), LOW, jnp.float32)

    def send_back(c, *slots):
        for s in slots:

            def body(k, _, s=s):
                level_copy(s, c, k).start()
                back_copy(s, c, k).start()
                return 0

            lax.fori_loop(1, PLANE, body, 0)

    send_out(0, 0)
    send_out(0, 1)
    odd = lax.rem(me, 2)
    partner = (me + 1 - 2 * odd, core)
    pair = [
        remote(ck_ref, pk, xp_send.at[0], xp_recv.at[0], partner),
        remote(cvt, pvt, xp_send.at[1], xp_recv.at[1], partner),
    ]

    @pl.when(odd == 0)
    def _():
        for copy in pair:
            copy.start()
        pvt[...] = jnp.zeros_like(pvt)


    for v in range(KV):
        value_copy(v).wait()

        def turn(w, _, v=v):
            vbuf[v * OWNED + w] = vstage[v % 2, w].T
            return 0

        lax.fori_loop(0, OWNED, turn, 0)
        if v + 2 < KV:
            value_copy(v + 2).start()

    z_codes.wait_recv()

    def p_code(k):
        return remote(
            zcode.at[:, :, pl.ds(0, OWNERS)], pcode.at[k], pc_send, pc_recv, in_plane(k)
        )

    def start_p_code(k, _):
        p_code(k).start()
        return 0

    lax.fori_loop(1, PLANE, start_p_code, 0)
    pcode[0] = zcode[:, :, :OWNERS]
    z_to_smem = pltpu.make_async_copy(zcode, zsm, sm_sem.at[0])
    z_to_smem.start()
    z_to_smem.wait()

    arrive((1, 0), (7, 0))

    @pl.when(odd == 1)
    def _():
        for copy in pair:
            copy.wait_recv()


    def own(h, _):
        v = h // GROUP
        lanes = pl.ds(pl.multiple_of(v * HEAD_SIZE, HEAD_SIZE), HEAD_SIZE)
        queries = jnp.concatenate([zq[0][0][h], zq[0][1][h]], axis=1)
        before = jnp.dot(pk[:, lanes], queries, preferred_element_type=jnp.float32)
        here = jnp.dot(ck_ref[:, lanes], queries, preferred_element_type=jnp.float32)
        key_pos = lax.broadcasted_iota(jnp.int32, (ROWS, ROWS), 0)
        query_pos = lax.broadcasted_iota(jnp.int32, (ROWS, ROWS), 1)
        before = jnp.where(odd == 1, before, LOW)
        here = jnp.where(key_pos <= query_pos, here, LOW)
        top = jnp.maximum(
            jnp.max(before, axis=0, keepdims=True), jnp.max(here, axis=0, keepdims=True)
        )
        weights_before = jnp.exp2((before - top) * SCALE2)
        weights_here = jnp.exp2((here - top) * SCALE2)
        total = jnp.sum(weights_before, axis=0, keepdims=True) + jnp.sum(
            weights_here, axis=0, keepdims=True
        )
        out = jnp.dot(pvt[v], weights_before.astype(jnp.bfloat16), preferred_element_type=jnp.float32)
        out += jnp.dot(cvt[v], weights_here.astype(jnp.bfloat16), preferred_element_type=jnp.float32)
        out = out * (1.0 / total)
        level = top * SCALE + jnp.log(total)
        for c in range(2):
            own_o[c, h] = out[:, c * HALF : (c + 1) * HALF]
            own_l[c, pl.ds(h, 1), :] = level[:, c * HALF : (c + 1) * HALF]
        return 0

    lax.fori_loop(0, HEADS, own, 0, unroll=4)
    arrive((2, 0), (6, 0))

    remote(
        pcode.at[pl.ds(1, PLANE - 1)], pcode.at[pl.ds(1, PLANE - 1)], pc_send, pc_recv, in_plane(1)
    ).wait_recv()
    p_to_smem = pltpu.make_async_copy(pcode, rsm, sm_sem.at[1])
    p_to_smem.start()
    p_to_smem.wait()
    for v in range(KV):
        key_copy(v).wait()

    units(0, 0, None)
    units(1, 0, None)
    arrive((3, 0), (5, 0))
    start_ring(1)
    units(0, 1, 7)
    arrive((4, 0))
    units(0, 2, 6)
    arrive((1, 1), (7, 1))
    units(0, 4, None, True)
    units(0, 5, None, True)
    units(0, 3, None, True)
    arrive((2, 1), (6, 1))

    def pick(s, h, t):
        owner = zsm[s, 0, OWNERS + h * TOPK + t]
        dx = lax.rem(lax.rem(owner, NX) - x + NX, NX)
        dy = lax.rem(lax.div(owner, NX * NZ) - y + NY, NY)
        dz = lax.rem(lax.rem(lax.div(owner, NX), NZ) - z + NZ, NZ)
        away = lax.div(dz + NZ - 1, NZ)
        return away, (dx + NX * dy) * (1 - away)

    def gather_levels(s, c):
        others = pl.ds(1, PLANE - 1)
        remote(
            rl[s][c].at[others], rl[s][c].at[others], ls_send.at[s], ls_recv.at[s, c], in_plane(1)
        ).wait_recv()

        def body(h, _):
            for t in range(TOPK):
                away, k = pick(s, h, t)
                lt[s, c, t, pl.ds(h, 1), :] = rl[s][c][k + PLANE * away]
            return 0

        lax.fori_loop(0, HEADS, body, 0, unroll=16)

    def weigh(c, heads, levels):
        top = functools.reduce(jnp.maximum, levels)
        parts = [jnp.exp(level - top) for level in levels]
        total = functools.reduce(jnp.add, parts)
        inverse = 1.0 / total
        for i, part in enumerate(parts):
            wt[c, i, heads] = part * inverse
        return top + jnp.log(total)

    def picked_levels(s, c, heads):
        return [lt[s, c, t, heads, :] for t in range(TOPK)]

    def picked_sum(s, c, h):
        total = None
        for t in range(TOPK):
            _, k = pick(s, h, t)
            term = wt[c, t, pl.ds(h, 1), :] * ret[s][c][k].astype(jnp.float32)
            total = term if total is None else total + term
        return total

    def wait_back(s, c):
        remote(
            ret[s][c].at[pl.ds(1, PLANE - 1)], ret[s][c].at[pl.ds(1, PLANE - 1)],
            rs_send.at[s], rs_recv.at[s, c], in_plane(1),
        ).wait_recv()

    def sum_copies(s, c, step):
        to = s + step
        heads = pl.ds(0, HEADS)
        if s == NZ // 2:
            heads = pl.ds(0 if step > 0 else HEADS // 2, HEADS // 2)
        way = 0 if step > 0 else 1
        return [
            remote(
                zacc.at[s, c, heads], zacc.at[to, c, heads], za_send.at[way, s, c],
                za_recv.at[to, c], along_z(step),
            ),
            remote(
                zl.at[s, c, heads], zl.at[to, c, heads], zl_send.at[way, s, c],
                zl_recv.at[to, c], along_z(step),
            ),
        ]

    def steps_from(s):
        return (1, -1) if s == NZ // 2 else (-1,) if s < NZ // 2 else (1,)

    def wait_sum(s, c, step):
        for copy in sum_copies(s - step, c, step):
            copy.wait_recv()

    def combine(c, s):
        gather_levels(s, c)
        wait_back(s, c)
        half = HEADS // 2
        if s == NZ // 2:
            parts = [(0, HEADS, False)]
        elif s == NZ // 2 + 1:
            parts = [(half, half, False), (0, half, True)]
        elif s == NZ // 2 - 1:
            parts = [(0, half, False), (half, half, True)]
        else:
            parts = [(0, HEADS, True)]
        for start, count, upstream in parts:
            heads = slice(start, start + count)
            levels = picked_levels(s, c, heads)
            if upstream:
                wait_sum(s, c, 1 if s > NZ // 2 else -1)
                levels.append(zl[s, c, heads])
            zl[s, c, heads] = weigh(c, heads, levels)

            def body(h, _, upstream=upstream):
                total = picked_sum(s, c, h)
                if upstream:
                    total += wt[c, TOPK, pl.ds(h, 1), :] * zacc[s, c, h].astype(jnp.float32)
                zacc[s, c, h] = total.astype(jnp.bfloat16)
                return 0

            lax.fori_loop(start, start + count, body, 0, unroll=8)
        for step in steps_from(s):
            for copy in sum_copies(s, c, step):
                copy.start()

    combine(0, 4)
    arrive((3, 1), (5, 1))
    arrive((4, 1))
    units(1, 1, 7)
    combine(0, 5)
    combine(0, 3)
    send_back(0, 6, 2)
    units(1, 2, 6)
    units(1, 5, 3)
    units(1, 4, None, True)
    send_back(1, 5, 3)
    combine(0, 6)
    combine(0, 2)
    send_back(0, 7, 1)
    combine(1, 4)
    combine(1, 5)
    combine(1, 3)
    send_back(1, 6, 2)
    combine(0, 7)
    combine(0, 1)
    send_back(1, 7, 1)
    combine(1, 6)
    combine(1, 2)
    send_back(0, 0)
    send_back(1, 0)
    combine(1, 7)
    combine(1, 1)
    for c in range(2):
        gather_levels(0, c)
        wait_back(0, c)
        wait_sum(0, c, -1)
        wait_sum(NZ, c, 1)
        every = slice(0, HEADS)
        weigh(c, every, picked_levels(0, c, every) + [zl[0, c], zl[NZ, c], own_l[c]])

        def finish(h, _, c=c):
            total = picked_sum(0, c, h)
            total += wt[c, TOPK, pl.ds(h, 1), :] * zacc[0, c, h].astype(jnp.float32)
            total += wt[c, TOPK + 1, pl.ds(h, 1), :] * zacc[NZ, c, h].astype(jnp.float32)
            total += wt[c, TOPK + 2, pl.ds(h, 1), :] * own_o[c, h]
            lanes = pl.ds(pl.multiple_of(h * HEAD_SIZE, HEAD_SIZE), HEAD_SIZE)
            out_ref[c * HALF : (c + 1) * HALF, lanes] = total.T.astype(jnp.bfloat16)
            return 0

        lax.fori_loop(0, HEADS, finish, 0, unroll=8)

    z_codes.wait_send()
    remote(
        pcode.at[pl.ds(1, PLANE - 1)], pcode.at[pl.ds(1, PLANE - 1)], pc_send, pc_recv, in_plane(1)
    ).wait_send()

    @pl.when(odd == 0)
    def _():
        for copy in pair:
            copy.wait_send()

    for c in range(2):
        for s in range(NZ):
            for step in (1, -1):
                if s == 0 or (s != NZ // 2 and (s < NZ // 2) == (step > 0)):
                    for part in parts_to(s, step):
                        z_query(s, c, step, part).wait_send()
            if s > 0:
                for step in steps_from(s):
                    for copy in sum_copies(s, c, step):
                        copy.wait_send()
    others = pl.ds(1, PLANE - 1)
    for s in range(NZ):
        remote(
            tx.at[s, :, others], rx.at[s, :, others], tx_send.at[s], rx_recv.at[s, 0, 0], in_plane(1)
        ).wait_send()
        remote(
            rx.at[s, :, others], tx.at[s, :, others], rs_send.at[s], rs_recv.at[s, 0], in_plane(1)
        ).wait_send()
        remote(
            lout.at[s, :, others], lout.at[s, :, others], ls_send.at[s], ls_recv.at[s, 0], in_plane(1)
        ).wait_send()


def exchange(q, ck, cv, kp, vp, code):
    dma = pltpu.SemaphoreType.DMA
    bf16, f32 = jnp.bfloat16, jnp.float32
    half = (HEADS, HEAD_SIZE, HALF)
    scratch = [pltpu.VMEM(half, bf16)] * (2 * NZ)
    scratch += [pltpu.VMEM((PLANE, HEAD_SIZE, HALF), bf16)] * (2 * NZ)
    scratch += [pltpu.VMEM((PLANE + 1, 1, HALF), f32)] * (2 * NZ)
    scratch += [
        pltpu.VMEM((KV * OWNED, KEY_BLOCK_SIZE, HEAD_SIZE), bf16),
        pltpu.VMEM((2, OWNED, KEY_BLOCK_SIZE, HEAD_SIZE), bf16),
        pltpu.VMEM((KV * OWNED, HEAD_SIZE, KEY_BLOCK_SIZE), bf16),
        pltpu.VMEM((NZ, 2, PLANE, HEAD_SIZE, HALF), bf16),
        pltpu.VMEM((NZ, 2, PLANE, HEAD_SIZE, HALF), bf16),
        pltpu.VMEM((NZ, 2, PLANE, 1, HALF), f32),
        pltpu.VMEM((NZ + 1, 2) + half, bf16),
        pltpu.VMEM((NZ + 1, 2, HEADS, HALF), f32),
        pltpu.VMEM((2,) + half, f32),
        pltpu.VMEM((2, HEADS, HALF), f32),
        pltpu.VMEM((ROWS, KV * HEAD_SIZE), bf16),
        pltpu.VMEM((KV, HEAD_SIZE, ROWS), bf16),
        pltpu.VMEM((KV, HEAD_SIZE, ROWS), bf16),
        pltpu.VMEM((NZ, 2, TOPK, HEADS, HALF), f32),
        pltpu.VMEM((2, TOPK + 3, HEADS, HALF), f32),
        pltpu.VMEM((NZ, 1, 2 * OWNERS), jnp.int32),
        pltpu.VMEM((PLANE, NZ, 1, OWNERS), jnp.int32),
        pltpu.SMEM((NZ, 1, 2 * OWNERS), jnp.int32),
        pltpu.SMEM((PLANE, NZ, 1, OWNERS), jnp.int32),
        dma((KV,)), dma((KV,)),
        dma((2, NZ, 2, 2)), dma((NZ, 2, 2)),
        dma, dma, dma, dma, dma((2,)),
        dma((2,)), dma((2,)),
        dma((NZ,)), dma((NZ, 2, PLANE)),
        dma((NZ,)), dma((NZ, 2)),
        dma((NZ,)), dma((NZ, 2)),
        dma((2, NZ, 2)), dma((NZ + 1, 2)), dma((2, NZ, 2)), dma((NZ + 1, 2)),
    ]
    vmem = pl.BlockSpec(memory_space=pltpu.VMEM)
    hbm = pl.BlockSpec(memory_space=pl.ANY)
    return pl.pallas_call(
        kernel,
        out_shape=jax.ShapeDtypeStruct((ROWS, HEADS * HEAD_SIZE), bf16),
        in_specs=[vmem, vmem, vmem, hbm, hbm, vmem, pl.BlockSpec(memory_space=pltpu.SMEM)],
        out_specs=vmem,
        scratch_shapes=scratch,
        compiler_params=pltpu.CompilerParams(
            collective_id=0, has_side_effects=True, vmem_limit_bytes=62 << 20
        ),
        name="attend",
    )(q, ck, cv, kp, vp, code, code)


def local(queries, current_keys, current_values, cached_key_pages, cached_value_pages, picks):
    chosen = picks.reshape(HEADS * TOPK)
    owner = chosen // OWNED
    head = jnp.arange(HEADS * TOPK) // TOPK
    table = head // GROUP * OWNED + chosen % OWNED
    value = head + HEADS * table
    by_owner = jnp.sum(
        jnp.where(owner[None, :] == jnp.arange(OWNERS)[:, None], value[None, :], 0), axis=1
    )
    code = jnp.concatenate([by_owner, jnp.pad(owner, (0, OWNERS - HEADS * TOPK))])
    return exchange(
        queries,
        current_keys,
        current_values,
        cached_key_pages.reshape(OWNED, KEY_BLOCK_SIZE, KV * HEAD_SIZE),
        cached_value_pages.reshape(OWNED, KEY_BLOCK_SIZE, KV * HEAD_SIZE),
        code.reshape(1, 2 * OWNERS).astype(jnp.int32),
    )


def solution(mesh):
    placed = (
        P("ctx", "kvh"),
        P("ctx", "kvh"),
        P("ctx", "kvh"),
        P("ctx", "kvh"),
        P("ctx", "kvh"),
        P("ctx", "kvh", None),
    )
    return jax.shard_map(
        local, mesh=mesh, in_specs=placed, out_specs=P("ctx", "kvh"), check_vma=False
    )
```
